32 devices in a mesh: asset: 16 (over z, y, x), rhs: 2 (over core).
Axes of the slice: x: 2, y: 2, z: 4, core: 2. Of those that a mesh axis runs over, the one named last changes fastest.
Arguments:
- targets: float32 [16384, 256], P('asset', 'rhs'), may hold values from -27 to 27
- ridge: float32 [16384], P('asset'), may hold values from 0.8 to 2.5
- blocks: bfloat16 [128, 16, 128, 128], P('asset', None, 'rhs'), may hold values from -0.046875 to 0.046875
- col_index: int32 [128, 16], P('asset'), may hold values from 0 to 127, as said below
- row_length: int32 [128], P('asset'), may hold values from 8 to 16, as said below
Outputs:
- solution: float32 [16384, 256], P('asset', 'rhs')
- residual: float32 [16384, 256], P('asset', 'rhs')
The draws below stay inside these ranges and needn't reach their ends.
Inputs may be any that keep to these rules, and one draw needn't show every extreme that they name: `col_index`: the block columns of row i are distinct and lie within 8 blocks of i, counted cyclically modulo 128; slots at or past row_length[i] hold such columns too and are ignored. `row_length`: each aligned group of 8 block rows holds at least one row with 16 used slots.
All inputs are finite; a program needn't handle non-finite values.
Results may differ from the reference program's by a relative error of at most 0.0075.
Values may be sent and summed in bfloat16 or wider, within the bound.
No kernel may reach another device: no remote copies, remote signals or barrier semaphores. Data moves between devices by JAX's collectives and lax.ppermute only.
A program may use at most 64 MiB of HBM per device.

```python
import math
import jax
import jax.numpy as jnp
from jax import lax

BR_DEV = 8
MAXB = 16
BS = 128
ITERS = 3
NB = 128
ASSETS = 16384
RHS = 256


def draw_targets(key, part):
    key = jax.random.fold_in(key, 31)
    first = jax.random.fold_in(key, 0)
    ramp = (1.0 + 2.0 * jnp.arange(ASSETS, dtype=jnp.float32) / (ASSETS - 1))[:, None]
    values = jnp.clip(jax.random.normal(first, (ASSETS, RHS), jnp.float32), -4.0, 4.0) * ramp
    return values.astype(jnp.float32)


def draw_col_index(key, part):
    key = jax.random.fold_in(key, 17)
    count = 2 * BR_DEV + 1

    def one_row(row):
        order = jax.random.permutation(jax.random.fold_in(key, row), count)
        offsets = order[:MAXB].astype(jnp.int32) - BR_DEV
        return (row + offsets) % NB
    return jax.vmap(one_row)(jnp.arange(NB, dtype=jnp.int32)).astype(jnp.int32)


def draw_row_length(key, part):
    key = jax.random.fold_in(key, 23)
    first, second = jax.random.split(key)
    lengths = jax.random.randint(first, (NB,), MAXB // 2, MAXB + 1)
    picked = jax.random.randint(second, (NB // BR_DEV,), 0, BR_DEV)
    full_row = jnp.arange(NB) % BR_DEV == jnp.repeat(picked, BR_DEV)
    return jnp.where(full_row, MAXB, lengths).astype(jnp.int32)


def levels(rng, shape, cuts, smallest, high):
    loudness = 1.0
    for axis_at, blocks in cuts:
        heights = jax.random.uniform(jax.random.fold_in(jax.random.fold_in(rng, 6), axis_at), (blocks,), jnp.float32, smallest / len(cuts), high / len(cuts))
        loudness = loudness * jnp.repeat(jnp.exp(heights), shape[axis_at] // blocks).reshape((-1,) + (1,) * (len(shape) - 1 - axis_at))
    return loudness


def centred(key, dims, spread, limit, shards=(), kind=jnp.bfloat16):
    array = jax.random.normal(key, dims, jnp.float32) * spread
    if len(shards) > 0:
        array = levels(key, dims, shards, -0.22, 0.18) * array
    return jnp.clip(array, min=-limit, max=limit).astype(kind)


def setup_inputs(seed: int = 0) -> dict:
    seeds = jax.random.split(jax.random.key(seed), 6)
    targets = draw_targets(jax.random.fold_in(seeds[5], 71), 0)
    ridge = jnp.clip(jnp.exp(math.log(2.5) - 1.13943427 * jax.random.uniform(seeds[1], (ASSETS,), jnp.float32) ** levels(seeds[1], (ASSETS,), ((0, 16),), -0.2, 0.2)), 0.8, 2.5)
    blocks = centred(seeds[2], (NB, MAXB, BS, BS), (8 * MAXB * BS) ** -0.5, 0.046875, ((0, 16), (2, 2)))
    col_index = draw_col_index(jax.random.fold_in(seeds[5], 71), 0)
    row_length = draw_row_length(jax.random.fold_in(seeds[5], 71), 0)
    return {"targets": targets, "ridge": ridge, "blocks": blocks, "col_index": col_index, "row_length": row_length}


def reference(targets, ridge, blocks, col_index, row_length):
    nblocks = blocks.shape[0]
    slots = blocks.shape[1]
    width = blocks.shape[2]
    cols = targets.shape[1]
    used = jnp.arange(slots)[None, :] < row_length[:, None]
    masked = blocks * used[:, :, None, None].astype(jnp.bfloat16)

    def operate(field):
        rounded = lax.optimization_barrier(field.astype(jnp.bfloat16))
        vt = rounded.astype(jnp.float32).reshape(nblocks, width, cols)

        def forward_row(item):
            block_set, index = item
            return jnp.einsum('kab,kbn->an', block_set.astype(jnp.float32), vt[index],
                              precision=lax.Precision.HIGHEST)

        forward = lax.map(forward_row, (masked, col_index))

        def back_step(carry, item):
            block_set, index, row_vals = item
            part = jnp.einsum('kab,an->kbn', block_set.astype(jnp.float32), row_vals,
                              precision=lax.Precision.HIGHEST)
            return carry.at[index].add(part), None

        backward, unused = lax.scan(back_step, jnp.zeros((nblocks, width, cols), jnp.float32),
                                    (masked, col_index, vt))
        return ridge[:, None] * field + 0.5 * (forward + backward).reshape(nblocks * width, cols)

    solution = jnp.zeros_like(targets)
    residual = targets
    direction = targets
    norm_now = jnp.sum(residual * residual, axis=0)
    for step in range(ITERS):
        image = operate(direction)
        alpha = norm_now / jnp.sum(direction * image, axis=0)
        solution = solution + alpha * direction
        residual = residual - alpha * image
        norm_next = jnp.sum(residual * residual, axis=0)
        direction = residual + (norm_next / norm_now) * direction
        norm_now = norm_next
    return solution, residual
```

```python
import jax
import jax.numpy as jnp
from jax import lax
from jax.experimental import pallas as pl
from jax.experimental.pallas import tpu as pltpu
from jax.sharding import PartitionSpec as P

F32 = jnp.float32
BF16 = jnp.bfloat16
VMEM = pl.BlockSpec(memory_space=pltpu.VMEM)
SMEM = pl.BlockSpec(memory_space=pltpu.SMEM)
LIMIT = 24 * 1024 * 1024
NN = (((1,), (0,)), ((), ()))
NT = (((1,), (1,)), ((), ()))


def call(kernel, out_shape, args, smem=0):
    return pl.pallas_call(
        kernel,
        out_shape=out_shape,
        in_specs=[SMEM] * smem + [VMEM] * (len(args) - smem),
        out_specs=jax.tree.map(lambda _: VMEM, out_shape),
        compiler_params=pltpu.CompilerParams(vmem_limit_bytes=LIMIT),
    )(*args)


def column_sums(values, width):
    folded = values[:, :width]
    for at in range(width, values.shape[1], width):
        folded = folded + values[:, at : at + width]
    return jnp.sum(folded.T, axis=0, keepdims=True)


def prepare_kernel(targets_ref, base_ref, rounded_ref, moment_ref):
    width = moment_ref.shape[1]
    for at in range(0, targets_ref.shape[0], width):
        tile = targets_ref[at : at + width, :].T
        base_ref[:, at : at + width] = tile
        rounded_ref[:, at : at + width] = tile.astype(BF16)
    values = targets_ref[...]
    moment_ref[...] = jnp.sum(values * values, axis=0, keepdims=True)


def spread_kernel(place_ref, length_ref, offset_ref, *refs):
    parts, (before_ref, own_ref, after_ref) = refs[:-3], refs[-3:]
    rows, slots, height, _ = parts[0].shape
    for ref in (before_ref, own_ref, after_ref):
        ref[...] = jnp.zeros_like(ref)

    def one_row(row, carry):
        def one_slot(slot, inner):
            place = place_ref[row, slot]
            for part, ref in enumerate(parts):
                start = row * (height * len(parts)) + offset_ref[part]
                at = pl.ds(pl.multiple_of(start, height), height)
                for side, out in enumerate((before_ref, own_ref, after_ref)):

                    @pl.when(place // rows == side)
                    def _():
                        out[place % rows, at, :] = ref[row, slot]

            return inner

        return lax.fori_loop(0, length_ref[row], one_slot, carry)

    lax.fori_loop(0, rows, one_row, 0)


def columns(ref, first, last, rows):
    return jnp.concatenate([ref[c, rows, :] for c in range(first, last)], axis=1)


def products_kernel(before_ref, after_ref, v_ref, up_ref, down_ref):
    rows, _, width = before_ref.shape
    for j in range(0, rows, 2):
        out = slice(j * width, (j + 2) * width)
        low = slice(0, (j + 2) * width)
        up_ref[:, out] = lax.dot_general(
            v_ref[:, low], columns(before_ref, j, j + 2, low), NN, preferred_element_type=F32
        ).astype(BF16)
        high = slice(j * width, rows * width)
        down_ref[:, out] = lax.dot_general(
            v_ref[:, high], columns(after_ref, j, j + 2, high), NN, preferred_element_type=F32
        ).astype(BF16)


def local_kernel(own_ref, v_ref, out_ref):
    rows, _, width = own_ref.shape
    every = slice(0, rows * width)
    for j in range(0, rows, 2):
        out = slice(j * width, (j + 2) * width)
        out_ref[:, out] = lax.dot_general(
            v_ref[...], columns(own_ref, j, j + 2, every), NN, preferred_element_type=F32
        ) + lax.dot_general(
            v_ref[...], columns(own_ref, 0, rows, out), NT, preferred_element_type=F32
        )


def finish_kernel(
    before_ref, after_ref, ridge_ref, k_ref, local_ref, vb_ref, va_ref, qb_ref, qa_ref,
    next_ref, rounded_ref, moment_ref
):
    rows, _, width = before_ref.shape
    for j in range(0, rows, 2):
        out = slice(j * width, (j + 2) * width)
        matrix = jnp.concatenate(
            [columns(before_ref, j, rows, out), columns(after_ref, 0, j + 2, out)], axis=1
        )
        field = jnp.concatenate(
            [vb_ref[:, j * width :], va_ref[:, : (j + 2) * width]], axis=1
        )
        both = lax.dot_general(field, matrix, NT, preferred_element_type=F32)
        both = both + local_ref[:, out] + qb_ref[:, out].astype(F32) + qa_ref[:, out].astype(F32)
        value = ridge_ref[:, out] * k_ref[:, out] + 0.5 * both
        next_ref[:, out] = value
        rounded_ref[:, out] = value.astype(BF16)
    value = next_ref[...]
    moment_ref[0:1, :] = column_sums(k_ref[...] * value, width)
    moment_ref[1:2, :] = column_sums(value * value, width)


def share(above, below):
    return jnp.where(below == 0, 0.0, above / below)


def scalars(m, shift, iters):
    zero = jnp.zeros_like(m[0])
    solution = [zero] * iters
    residual = [zero + 1.0] + [zero] * iters
    direction = [zero + 1.0] + [zero] * (iters - 1)

    def inner(a, b):
        total = zero
        for i, left in enumerate(a):
            for j, right in enumerate(b):
                if i + j < len(m):
                    total = total + left * right * m[i + j]
        return total

    now = m[0]
    for step in range(iters):
        used = direction[: step + 1]
        image = [shift * value for value in used] + [zero]
        for i, value in enumerate(used):
            image[i + 1] = image[i + 1] + value
        alpha = share(now, inner(used, image))
        for i, value in enumerate(used):
            solution[i] = solution[i] + alpha * value
        for i, value in enumerate(image):
            residual[i] = residual[i] - alpha * value
        if step + 1 < iters:
            left = residual[: step + 2]
            new = inner(left, left)
            beta = share(new, now)
            direction = [r + beta * d for r, d in zip(residual[:iters], direction, strict=True)]
            now = new
    return solution, residual


def combine_kernel(shift_ref, moment_ref, targets_ref, k1_ref, k2_ref, k3_ref, solution_ref, residual_ref):
    width = moment_ref.shape[2]
    summed = moment_ref[0]
    for i in range(1, moment_ref.shape[0]):
        summed = summed + moment_ref[i]
    m = [summed[i : i + 1, :] for i in range(6)]
    x, r = scalars(m, shift_ref[0:1, :], 3)
    for at in range(0, targets_ref.shape[0], width):
        out = slice(at, at + width)
        k0 = targets_ref[out, :]
        k1, k2, k3 = k1_ref[:, out].T, k2_ref[:, out].T, k3_ref[:, out].T
        solution_ref[out, :] = x[0] * k0 + x[1] * k1 + x[2] * k2
        residual_ref[out, :] = r[0] * k0 + r[1] * k1 + r[2] * k2 + r[3] * k3


def moved(value, axis, distance):
    count = lax.axis_size(axis)
    return lax.ppermute(value, axis, [(i, (i + distance) % count) for i in range(count)])


def to_all(value, axis):
    count = lax.axis_size(axis)
    return lax.all_to_all(jnp.broadcast_to(value[None], (count,) + value.shape), axis, 0, 0)


def shards(targets, ridge, blocks, col_index, row_length):
    rows, slots, height, width = blocks.shape
    cols = targets.shape[1]
    assets = rows * width
    devices = lax.axis_size("asset")
    halves = lax.axis_size("rhs")
    start = lax.axis_index("asset") * rows
    place = (col_index - start + rows) % (rows * devices)
    if halves == 2:
        mine = lax.axis_index("rhs") * height
        parts = [blocks, moved(blocks, "rhs", 1)]
        offsets = jnp.stack([mine, height - mine]).astype(jnp.int32)
    else:
        parts = [lax.all_gather(blocks, "rhs", axis=2, tiled=True)]
        offsets = jnp.zeros((1,), jnp.int32)

    def shape(kind, *dims):
        return jax.ShapeDtypeStruct(dims, kind)

    field, rounded = shape(F32, cols, assets), shape(BF16, cols, assets)
    base, v, m0 = call(prepare_kernel, (field, rounded, shape(F32, 1, cols)), (targets,))
    sums = to_all(jnp.broadcast_to(jnp.sum(ridge), (1, 128)), "asset")
    shift = jnp.sum(sums, axis=0) / (devices * assets)
    shifted = ridge[None, :] - shift[0, 0]

    band = shape(BF16, rows, assets, width)
    before, own, after = call(
        spread_kernel, (band,) * 3, (place, row_length, offsets, *parts), smem=3
    )
    basis, moments = [base], [m0]
    for step in range(3):
        vb, va = moved(v, "asset", 1), moved(v, "asset", -1)
        up, down = call(products_kernel, (rounded,) * 2, (before, after, v))
        qa, qb = moved(up, "asset", -1), moved(down, "asset", 1)
        local = call(local_kernel, field, (own, v))
        following, v, pair = call(
            finish_kernel,
            (field, rounded, shape(F32, 2, cols)),
            (before, after, shifted, basis[-1], local, vb, va, qb, qa),
        )
        basis.append(following)
        moments.append(pair)
    gathered = to_all(jnp.concatenate(moments + [jnp.zeros((1, cols), F32)]), "asset")
    out = shape(F32, assets, cols)
    return call(combine_kernel, (out, out), (shift, gathered, targets, *basis[1:]))


def solution(mesh):
    return jax.shard_map(
        shards,
        mesh=mesh,
        in_specs=(
            P("asset", "rhs"),
            P("asset"),
            P("asset", None, "rhs", None),
            P("asset", None),
            P("asset"),
        ),
        out_specs=(P("asset", "rhs"), P("asset", "rhs")),
        check_vma=False,
    )
```

```python
import jax
import jax.numpy as jnp
from jax import lax
from jax.experimental import pallas as pl
from jax.experimental.pallas import tpu as pltpu
from jax.sharding import PartitionSpec as P

F32 = jnp.float32
BF16 = jnp.bfloat16
VMEM = pl.BlockSpec(memory_space=pltpu.VMEM)
SMEM = pl.BlockSpec(memory_space=pltpu.SMEM)
LIMIT = 8 * 1024 * 1024
HBM = pl.BlockSpec(memory_space=pltpu.HBM)
NN = (((1,), (0,)), ((), ()))
NT = (((1,), (1,)), ((), ()))


def call(kernel, out_shape, args, smem=0, outside=(), scratch=(), aliases=None):
    specs = [SMEM] * smem + [VMEM] * (len(args) - smem)
    for at in outside:
        specs[at] = HBM
    return pl.pallas_call(
        kernel,
        out_shape=out_shape,
        in_specs=specs,
        out_specs=jax.tree.map(lambda _: VMEM, out_shape),
        scratch_shapes=scratch,
        input_output_aliases=aliases or {},
        compiler_params=pltpu.CompilerParams(vmem_limit_bytes=LIMIT),
    )(*args)


def column_sums(values, width):
    folded = values[:, :width]
    for at in range(width, values.shape[1], width):
        folded = folded + values[:, at : at + width]
    return jnp.sum(folded.T, axis=0, keepdims=True)


def prepare_kernel(targets_ref, ridge_ref, base_ref, message_ref, moment_ref):
    assets, cols = targets_ref.shape
    width = moment_ref.shape[1]
    for at in range(0, assets, width):
        tile = targets_ref[at : at + width, :].T
        base_ref[:, at : at + width] = tile
        message_ref[:cols, at : at + width] = tile.astype(BF16)
    values = targets_ref[...]
    moment_ref[...] = jnp.sum(values * values, axis=0, keepdims=True)
    mean = jnp.sum(ridge_ref[...], axis=1, keepdims=True) / assets
    rest = message_ref.shape[0] - cols
    message_ref[cols:, :] = jnp.broadcast_to(mean, (rest, assets)).astype(BF16)


def place_blocks(col_ref, length_ref, offset, part_ref, band_ref):
    rows, slots, height, width = part_ref.shape
    spare = band_ref.shape[0] - 1
    total = rows * lax.axis_size("asset")
    first = lax.axis_index("asset") * rows - rows

    def one_row(row, carry):
        at = pl.ds(pl.multiple_of(row * width + offset, height), height)
        for slot in range(slots):
            place = col_ref[row, slot] - first
            place = jnp.where(place < 0, place + total, place)
            place = jnp.where(place >= total, place - total, place)
            place = jnp.where(slot < length_ref[row], place, spare)
            band_ref[place, at, :] = part_ref[row, slot]
        return carry

    lax.fori_loop(0, rows, one_row, 0)


def spread_first_kernel(col_ref, length_ref, part_ref, band_ref):
    band_ref[...] = jnp.zeros_like(band_ref)
    height = part_ref.shape[2]
    mine = 0 if height == part_ref.shape[3] else lax.axis_index("rhs") * height
    place_blocks(col_ref, length_ref, mine, part_ref, band_ref)


def spread_other_kernel(col_ref, length_ref, part_ref, _, band_ref):
    height = part_ref.shape[2]
    place_blocks(col_ref, length_ref, (1 - lax.axis_index("rhs")) * height, part_ref, band_ref)


def is_odd(dims):
    return jnp.full(dims, lax.axis_index("asset") % 2, jnp.int32) == 1


def columns(ref, first, last, rows):
    return jnp.concatenate([ref[c, rows, :] for c in range(first, last)], axis=1)


def products_kernel(band_ref, v_ref, near_ref, far_ref):
    places, _, width = band_ref.shape
    rows = places // 3
    cols = near_ref.shape[0]
    odd = is_odd((cols, 2 * width))
    for j in range(0, rows, 2):
        out = slice(j * width, (j + 2) * width)
        low = slice(0, (j + 2) * width)
        high = slice(j * width, rows * width)
        before = lax.dot_general(
            v_ref[:cols, low], columns(band_ref, j, j + 2, low), NN, preferred_element_type=F32
        )
        after = lax.dot_general(
            v_ref[:cols, high],
            columns(band_ref, 2 * rows + j, 2 * rows + j + 2, high),
            NN,
            preferred_element_type=F32,
        )
        near_ref[:, out] = jnp.where(odd, before, after).astype(BF16)
        far_ref[:, out] = jnp.where(odd, after, before).astype(BF16)


def products_third_kernel(
    band_ref, shift_ref, mean_ref, near1_ref, far1_ref, v_ref, near_ref, far_ref, near2_ref, far2_ref
):
    products_kernel(band_ref, v_ref, near2_ref, far2_ref)
    gap = 2 * (mean_ref[0:1, 0:1] - shift_ref[0:1, 0:1])
    near_ref[...] = (near2_ref[...].astype(F32) + gap * near1_ref[...].astype(F32)).astype(BF16)
    far_ref[...] = (far2_ref[...].astype(F32) + gap * far1_ref[...].astype(F32)).astype(BF16)


def local_kernel(band_ref, v_ref, out_ref):
    places, _, width = band_ref.shape
    rows = places // 3
    cols = out_ref.shape[0]
    every = slice(0, rows * width)
    for j in range(0, rows, 2):
        out = slice(j * width, (j + 2) * width)
        out_ref[:, out] = lax.dot_general(
            v_ref[:cols, :],
            columns(band_ref, rows + j, rows + j + 2, every),
            NN,
            preferred_element_type=F32,
        ) + lax.dot_general(
            v_ref[:cols, :], columns(band_ref, rows, 2 * rows, out), NT, preferred_element_type=F32
        )


def neighbours(near_ref, far_ref, cols):
    near, far = near_ref[:cols, :].astype(F32), far_ref[:cols, :].astype(F32)
    odd = is_odd(near.shape)
    return jnp.where(odd, near, far).astype(BF16), jnp.where(odd, far, near).astype(BF16)


def forward_products(band_ref, before, after, j):
    places, _, width = band_ref.shape
    rows = places // 3
    out = slice(j * width, (j + 2) * width)
    return out, lax.dot_general(
        before[:, j * width :], columns(band_ref, j, rows, out), NT, preferred_element_type=F32
    ), lax.dot_general(
        after[:, : (j + 2) * width],
        columns(band_ref, 2 * rows, 2 * rows + j + 2, out),
        NT,
        preferred_element_type=F32,
    )


def cross_first_kernel(
    band_ref, ridge_ref, k_ref, local_ref, own_ref, near_ref, far_ref,
    sum_ref, before_ref, after_ref, mean_ref
):
    cols, width = k_ref.shape[0], mean_ref.shape[1]
    before, after = neighbours(near_ref, far_ref, cols)
    means = [ref[cols : cols + 8, :width].astype(F32)[:1] for ref in (own_ref, near_ref, far_ref)]
    odd = is_odd(means[0].shape)
    means += [jnp.where(odd, means[1], means[2]), jnp.where(odd, means[2], means[1])]
    means.append(means[0] + means[1])
    for i, value in enumerate(means):
        mean_ref[i : i + 1, :] = value
    for j in range(0, band_ref.shape[0] // 3, 2):
        out, first, second = forward_products(band_ref, before, after, j)
        before_ref[:, out] = first
        after_ref[:, out] = second
        sum_ref[:, out] = ridge_ref[:, out] * k_ref[:, out] + 0.5 * (local_ref[:, out] + first + second)


def finish_first_kernel(k_ref, mean_ref, sum_ref, near_ref, far_ref, next_ref, rounded_ref):
    value = sum_ref[...] + 0.5 * (near_ref[...].astype(F32) + far_ref[...].astype(F32))
    next_ref[...] = value
    rounded_ref[...] = (value - mean_ref[0:1, 0:1] * k_ref[...]).astype(BF16)


def cross_second_kernel(
    band_ref, ridge_ref, mean_ref, k_ref, local0_ref, local_ref, before0_ref, after0_ref, qn0_ref, qf0_ref,
    near_ref, far_ref, sum_ref, before_ref, after_ref
):
    own, mean_near, mean_far, mean_before, mean_after = (mean_ref[i : i + 1, 0:1] for i in range(5))
    before, after = neighbours(near_ref, far_ref, k_ref.shape[0])
    for j in range(0, band_ref.shape[0] // 3, 2):
        out, first, second = forward_products(band_ref, before, after, j)
        before_ref[:, out] = first
        after_ref[:, out] = second
        known = own * local0_ref[:, out] + mean_before * before0_ref[:, out] + mean_after * after0_ref[:, out]
        known = known + mean_near * qn0_ref[:, out].astype(F32) + mean_far * qf0_ref[:, out].astype(F32)
        both = local_ref[:, out] + first + second + known
        sum_ref[:, out] = ridge_ref[:, out] * k_ref[:, out] + 0.5 * both


def finish_second_kernel(k0_ref, k_ref, mean_ref, sum_ref, q_ref, next_ref, rounded_ref):
    value = sum_ref[...] + 0.5 * q_ref[...].astype(F32)
    next_ref[...] = value
    own = mean_ref[0:1, 0:1]
    rounded_ref[...] = (value - 2 * own * k_ref[...] + own * own * k0_ref[...]).astype(BF16)


def settle_kernel(shift_ref, k0_ref, k1_ref, k2_ref, s1_ref, s2_ref, moment_ref):
    width = moment_ref.shape[1]
    c = shift_ref[0:1, 0:1]
    k0, k1 = k0_ref[...], k1_ref[...]
    s1 = k1 - c * k0
    s2 = k2_ref[...] - 2 * c * k1 + c * c * k0
    s1_ref[...] = s1
    s2_ref[...] = s2
    for i, value in enumerate((k0 * s1, s1 * s1, s1 * s2, s2 * s2)):
        moment_ref[i : i + 1, :] = column_sums(value, width)


def cross_third_kernel(
    band_ref, ridge_ref, shift_ref, mean_ref, k_ref, local0_ref, local1_ref, local_ref,
    before0_ref, before1_ref, after0_ref, after1_ref, qn0_ref, qf0_ref,
    near_ref, far_ref, sum_ref, form_ref
):
    width = form_ref.shape[1]
    c = shift_ref[0:1, 0:1]
    own, mean_near, mean_far, mean_before, mean_after = (mean_ref[i : i + 1, 0:1] - c for i in range(5))
    before, after = neighbours(near_ref, far_ref, k_ref.shape[0])
    form = jnp.zeros((k_ref.shape[0], width), F32)

    def known(gap, zeroth_ref, first_ref, out):
        zeroth, first = zeroth_ref[:, out].astype(F32), first_ref[:, out].astype(F32)
        return 2 * gap * first + gap * gap * zeroth

    for j in range(0, band_ref.shape[0] // 3, 2):
        out, first, second = forward_products(band_ref, before, after, j)
        first = first + known(mean_before, before0_ref, before1_ref, out)
        second = second + known(mean_after, after0_ref, after1_ref, out)
        local = local_ref[:, out] + known(own, local0_ref, local1_ref, out)
        back = mean_near * mean_near * qn0_ref[:, out].astype(F32)
        back = back + mean_far * mean_far * qf0_ref[:, out].astype(F32)
        mine = (ridge_ref[:, out] - c) * k_ref[:, out] + 0.5 * local
        sum_ref[:, out] = mine + 0.5 * (first + second + back)
        part = k_ref[:, out] * (mine + first + second)
        form = form + part[:, :width] + part[:, width:]
    form_ref[...] = jnp.sum(form.T, axis=0, keepdims=True)


def finish_third_kernel(sum_ref, q_ref, next_ref):
    next_ref[...] = sum_ref[...] + 0.5 * q_ref[...].astype(F32)


def share(above, below):
    return jnp.where(below == 0, 0.0, above / below)


def scalars(m, shift, iters):
    zero = jnp.zeros_like(m[0])
    solution = [zero] * iters
    residual = [zero + 1.0] + [zero] * iters
    direction = [zero + 1.0] + [zero] * (iters - 1)

    def inner(a, b):
        total = zero
        for i, left in enumerate(a):
            for j, right in enumerate(b):
                if i + j < len(m):
                    total = total + left * right * m[i + j]
        return total

    now = m[0]
    for step in range(iters):
        used = direction[: step + 1]
        image = [shift * value for value in used] + [zero]
        for i, value in enumerate(used):
            image[i + 1] = image[i + 1] + value
        alpha = share(now, inner(used, image))
        for i, value in enumerate(used):
            solution[i] = solution[i] + alpha * value
        for i, value in enumerate(image):
            residual[i] = residual[i] - alpha * value
        if step + 1 < iters:
            left = residual[: step + 2]
            new = inner(left, left)
            beta = share(new, now)
            direction = [r + beta * d for r, d in zip(residual[:iters], direction, strict=True)]
            now = new
    return solution, residual


def combine_kernel(shift_ref, moment_ref, targets_ref, k1_ref, k2_ref, k3_ref, solution_ref, residual_ref):
    width = moment_ref.shape[1]
    m = [moment_ref[i : i + 1, :] for i in range(6)]
    x, r = scalars(m, shift_ref[...], 3)
    for at in range(0, targets_ref.shape[0], width):
        out = slice(at, at + width)
        k0 = targets_ref[out, :]
        k1, k2, k3 = k1_ref[:, out].T, k2_ref[:, out].T, k3_ref[:, out].T
        solution_ref[out, :] = x[0] * k0 + x[1] * k1 + x[2] * k2
        residual_ref[out, :] = r[0] * k0 + r[1] * k1 + r[2] * k2 + r[3] * k3


def near(value):
    count = lax.axis_size("asset")
    return lax.ppermute(value, "asset", [(i, i ^ 1) for i in range(count)])


def far(value):
    count = lax.axis_size("asset")
    return lax.ppermute(
        value, "asset", [(i, (i + 1 if i % 2 else i - 1) % count) for i in range(count)]
    )


def back(value):
    count = lax.axis_size("asset")
    return lax.ppermute(
        value, "asset", [(i, (i + 2 if i % 2 else i - 2) % count) for i in range(count)]
    )


def joined(to_near, to_far):
    return near((to_near.astype(F32) + back(to_far).astype(F32)).astype(BF16))


def sum_step(value, axis, distance):
    count = lax.axis_size(axis)
    return value + lax.ppermute(value, axis, [(i, i ^ distance) for i in range(count)])


def sum_over(value, axis):
    count = lax.axis_size(axis)
    step = 1
    while step < count:
        total = value
        for distance in (step, 2 * step, 3 * step) if 2 * step < count else (step,):
            route = [(i, i ^ distance) for i in range(count)]
            total = total + lax.ppermute(value, axis, route)
        value = total
        step *= 4
    return value


def together(*values):
    return lax.optimization_barrier(values)


def shards(targets, ridge, blocks, col_index, row_length):
    rows, slots, height, width = blocks.shape
    cols = targets.shape[1]
    assets = rows * width
    devices = lax.axis_size("asset")
    halves = lax.axis_size("rhs")
    ridge = ridge[None, :]

    def shape(kind, *dims):
        return jax.ShapeDtypeStruct(dims, kind)

    field, rounded, row = shape(F32, cols, assets), shape(BF16, cols, assets), shape(F32, 1, cols)
    band_shape = shape(BF16, 3 * rows + 1, assets, width)
    if halves == 2:
        part, other = blocks, lax.ppermute(blocks, "rhs", [(0, 1), (1, 0)])
    else:
        part, other = lax.all_gather(blocks, "rhs", axis=2, tiled=True), None

    k0, v0, m0 = call(prepare_kernel, (field, shape(BF16, cols + 16, assets), row), (targets, ridge))
    near0, far0 = near(v0), far(v0)
    band = call(spread_first_kernel, band_shape, (col_index, row_length, part), smem=2)
    if other is not None:
        band = call(
            spread_other_kernel, band_shape, (col_index, row_length, other, band), smem=2, aliases={3: 0}
        )
    distances = [1 << i for i in range(1, (devices - 1).bit_length())]
    pieces = (field,) * 3

    to_near, to_far = call(products_kernel, (rounded,) * 2, (band, v0))
    qf0, qn0 = far(to_far), near(to_near)
    local0 = call(local_kernel, field, (band, v0))
    partial, before0, after0, means = call(
        cross_first_kernel,
        (*pieces, shape(F32, 8, width)),
        (band, ridge, k0, local0, v0, near0, far0),
    )
    mean = sum_step(means[5:6], "asset", distances[0])
    mean, partial = together(mean, partial)
    k1, v1 = call(finish_first_kernel, (field, rounded), (k0, means, partial, qn0, qf0))

    to_near1, to_far1 = call(products_kernel, (rounded,) * 2, (band, v1))
    far1, near1 = far(v1), near(v1)
    q1 = joined(to_near1, to_far1)
    local1 = call(local_kernel, field, (band, v1))
    mean, _ = together(mean, v1)
    for distance in distances[1:-1]:
        mean = sum_step(mean, "asset", distance)
    partial, before1, after1 = call(
        cross_second_kernel,
        pieces,
        (band, ridge, means, k1, local0, local1, before0, after0, qn0, qf0, near1, far1),
    )
    mean, _ = together(mean, partial)
    shift = sum_step(mean, "asset", distances[-1]) / devices
    k2, v2 = call(finish_second_kernel, (field, rounded), (k0, k1, means, partial, q1))

    far2, near2 = far(v2), near(v2)
    to_near, to_far, _, _ = call(
        products_third_kernel, (rounded,) * 4, (band, shift, means, to_near1, to_far1, v2)
    )
    q2 = joined(to_near, to_far)
    local2 = call(local_kernel, field, (band, v2))
    s1, s2, pairs = call(settle_kernel, (field, field, shape(F32, 4, cols)), (shift, k0, k1, k2))
    partial, form = call(
        cross_third_kernel,
        (field, row),
        (
            band, ridge, shift, means, s2, local0, local1, local2, before0, before1, after0, after1,
            qn0, qf0, near2, far2,
        ),
    )
    moments = sum_over(jnp.concatenate([m0, pairs, form]), "asset")
    s3 = call(finish_third_kernel, field, (partial, q2))
    out = shape(F32, assets, cols)
    return call(combine_kernel, (out, out), (shift, moments, targets, s1, s2, s3))


def solution(mesh):
    return jax.shard_map(
        shards,
        mesh=mesh,
        in_specs=(
            P("asset", "rhs"),
            P("asset"),
            P("asset", None, "rhs", None),
            P("asset", None),
            P("asset"),
        ),
        out_specs=(P("asset", "rhs"), P("asset", "rhs")),
        check_vma=False,
    )
```

```python
import jax
import jax.numpy as jnp
from jax import lax
from jax.experimental import pallas as pl
from jax.experimental.pallas import tpu as pltpu
from jax.sharding import PartitionSpec as P

F32 = jnp.float32
BF16 = jnp.bfloat16
VMEM = pl.BlockSpec(memory_space=pltpu.VMEM)
SMEM = pl.BlockSpec(memory_space=pltpu.SMEM)
LIMIT = 8 * 1024 * 1024
HBM = pl.BlockSpec(memory_space=pltpu.HBM)
NN = (((1,), (0,)), ((), ()))
NT = (((1,), (1,)), ((), ()))


def call(kernel, out_shape, args, smem=0, outside=(), scratch=(), aliases=None, flops=0):
    specs = [SMEM] * smem + [VMEM] * (len(args) - smem)
    for at in outside:
        specs[at] = HBM
    return pl.pallas_call(
        kernel,
        out_shape=out_shape,
        in_specs=specs,
        out_specs=jax.tree.map(lambda _: VMEM, out_shape),
        scratch_shapes=scratch,
        input_output_aliases=aliases or {},
        cost_estimate=pl.CostEstimate(flops=flops, bytes_accessed=2**20, transcendentals=0) if flops else None,
        compiler_params=pltpu.CompilerParams(vmem_limit_bytes=LIMIT),
    )(*args)


def column_sums(values, width):
    folded = values[:, :width]
    for at in range(width, values.shape[1], width):
        folded = folded + values[:, at : at + width]
    return jnp.sum(folded.T, axis=0, keepdims=True)


def prepare_kernel(targets_ref, base_ref, rounded_ref, moment_ref):
    assets = targets_ref.shape[0]
    width = moment_ref.shape[1]
    for at in range(0, assets, width):
        tile = targets_ref[at : at + width, :].T
        base_ref[:, at : at + width] = tile
        rounded_ref[:, at : at + width] = tile.astype(BF16)
    values = targets_ref[...]
    moment_ref[...] = jnp.sum(values * values, axis=0, keepdims=True)


def place_blocks(col_ref, length_ref, offset, part_ref, band_ref):
    rows, slots, height, width = part_ref.shape
    spare = band_ref.shape[0] - 1
    total = rows * lax.axis_size("asset")
    first = lax.axis_index("asset") * rows - rows

    def one_row(row, carry):
        at = pl.ds(pl.multiple_of(row * width + offset, height), height)
        for slot in range(slots):
            place = col_ref[row, slot] - first
            place = jnp.where(place < 0, place + total, place)
            place = jnp.where(place >= total, place - total, place)
            place = jnp.where(slot < length_ref[row], place, spare)
            band_ref[place, at, :] = part_ref[row, slot]
        return carry

    lax.fori_loop(0, rows, one_row, 0)


def spread_first_kernel(col_ref, length_ref, part_ref, band_ref):
    band_ref[...] = jnp.zeros_like(band_ref)
    height = part_ref.shape[2]
    mine = 0 if height == part_ref.shape[3] else lax.axis_index("rhs") * height
    place_blocks(col_ref, length_ref, mine, part_ref, band_ref)


def spread_other_kernel(col_ref, length_ref, part_ref, _, band_ref):
    height = part_ref.shape[2]
    place_blocks(col_ref, length_ref, (1 - lax.axis_index("rhs")) * height, part_ref, band_ref)


def is_odd(dims):
    return jnp.full(dims, lax.axis_index("asset") % 2, jnp.int32) == 1


def columns(ref, first, last, rows):
    return jnp.concatenate([ref[c, rows, :] for c in range(first, last)], axis=1)


def products_kernel(band_ref, v_ref, near_ref, far_ref):
    places, _, width = band_ref.shape
    rows = places // 3
    cols = v_ref.shape[0]
    odd = is_odd((cols, 2 * width))
    for j in range(0, rows, 2):
        out = slice(j * width, (j + 2) * width)
        low = slice(0, (j + 2) * width)
        high = slice(j * width, rows * width)
        before = lax.dot_general(
            v_ref[:, low], columns(band_ref, j, j + 2, low), NN, preferred_element_type=F32
        )
        after = lax.dot_general(
            v_ref[:, high],
            columns(band_ref, 2 * rows + j, 2 * rows + j + 2, high),
            NN,
            preferred_element_type=F32,
        )
        near_ref[:cols, out] = jnp.where(odd, before, after).astype(BF16)
        far_ref[:cols, out] = jnp.where(odd, after, before).astype(BF16)


def products_first_kernel(band_ref, v_ref, ridge_ref, near_ref, far_ref):
    products_kernel(band_ref, v_ref, near_ref, far_ref)
    cols, assets = v_ref.shape
    mean = jnp.sum(ridge_ref[...], axis=1, keepdims=True) / assets
    rest = jnp.broadcast_to(mean, (near_ref.shape[0] - cols, assets)).astype(BF16)
    near_ref[cols:, :] = rest
    far_ref[cols:, :] = rest


def products_third_kernel(
    band_ref, shift_ref, mean_ref, near1_ref, far1_ref, v_ref, near_ref, far_ref, near2_ref, far2_ref
):
    products_kernel(band_ref, v_ref, near2_ref, far2_ref)
    gap = 2 * (mean_ref[0:1, 0:1] - shift_ref[0:1, 0:1])
    near_ref[...] = (near2_ref[...].astype(F32) + gap * near1_ref[...].astype(F32)).astype(BF16)
    far_ref[...] = (far2_ref[...].astype(F32) + gap * far1_ref[...].astype(F32)).astype(BF16)


def local_kernel(band_ref, v_ref, out_ref):
    places, _, width = band_ref.shape
    rows = places // 3
    cols = out_ref.shape[0]
    every = slice(0, rows * width)
    for j in range(0, rows, 2):
        out = slice(j * width, (j + 2) * width)
        out_ref[:, out] = lax.dot_general(
            v_ref[:cols, :],
            columns(band_ref, rows + j, rows + j + 2, every),
            NN,
            preferred_element_type=F32,
        ) + lax.dot_general(
            v_ref[:cols, :], columns(band_ref, rows, 2 * rows, out), NT, preferred_element_type=F32
        )


def neighbours(near_ref, far_ref, cols):
    near, far = near_ref[:cols, :].astype(F32), far_ref[:cols, :].astype(F32)
    odd = is_odd(near.shape)
    return jnp.where(odd, near, far).astype(BF16), jnp.where(odd, far, near).astype(BF16)


def forward_products(band_ref, before, after, j):
    places, _, width = band_ref.shape
    rows = places // 3
    out = slice(j * width, (j + 2) * width)
    return out, lax.dot_general(
        before[:, j * width :], columns(band_ref, j, rows, out), NT, preferred_element_type=F32
    ), lax.dot_general(
        after[:, : (j + 2) * width],
        columns(band_ref, 2 * rows, 2 * rows + j + 2, out),
        NT,
        preferred_element_type=F32,
    )


def gather_first_kernel(ridge_ref, k_ref, local_ref, own_ref, near_ref, far_ref, sum_ref, mean_ref):
    cols, width = k_ref.shape[0], mean_ref.shape[1]
    means = [ref[cols : cols + 8, :width].astype(F32)[:1] for ref in (own_ref, near_ref, far_ref)]
    odd = is_odd(means[0].shape)
    means += [jnp.where(odd, means[1], means[2]), jnp.where(odd, means[2], means[1])]
    means.append(means[0] + means[1])
    for i, value in enumerate(means):
        mean_ref[i : i + 1, :] = value
    both = local_ref[...] + near_ref[:cols, :].astype(F32) + far_ref[:cols, :].astype(F32)
    sum_ref[...] = ridge_ref[...] * k_ref[...] + 0.5 * both


def cross_first_kernel(
    band_ref, sum_ref, k_ref, mean_ref, near_ref, far_ref, next_ref, rounded_ref, before_ref, after_ref
):
    before, after = neighbours(near_ref, far_ref, k_ref.shape[0])
    for j in range(0, band_ref.shape[0] // 3, 2):
        out, first, second = forward_products(band_ref, before, after, j)
        before_ref[:, out] = first
        after_ref[:, out] = second
        value = sum_ref[:, out] + 0.5 * (first + second)
        next_ref[:, out] = value
        rounded_ref[:, out] = (value - mean_ref[0:1, 0:1] * k_ref[:, out]).astype(BF16)


def cross_second_kernel(
    band_ref, ridge_ref, mean_ref, k_ref, local0_ref, local_ref, before0_ref, after0_ref, qn0_ref, qf0_ref,
    near_ref, far_ref, sum_ref, before_ref, after_ref
):
    own, mean_near, mean_far, mean_before, mean_after = (mean_ref[i : i + 1, 0:1] for i in range(5))
    before, after = neighbours(near_ref, far_ref, k_ref.shape[0])
    for j in range(0, band_ref.shape[0] // 3, 2):
        out, first, second = forward_products(band_ref, before, after, j)
        before_ref[:, out] = first
        after_ref[:, out] = second
        known = own * local0_ref[:, out] + mean_before * before0_ref[:, out] + mean_after * after0_ref[:, out]
        known = known + mean_near * qn0_ref[: k_ref.shape[0], out].astype(F32) + mean_far * qf0_ref[: k_ref.shape[0], out].astype(F32)
        both = local_ref[:, out] + first + second + known
        sum_ref[:, out] = ridge_ref[:, out] * k_ref[:, out] + 0.5 * both


def finish_second_kernel(k0_ref, k_ref, mean_ref, sum_ref, q_ref, next_ref, rounded_ref):
    value = sum_ref[...] + 0.5 * q_ref[...].astype(F32)
    next_ref[...] = value
    own = mean_ref[0:1, 0:1]
    rounded_ref[...] = (value - 2 * own * k_ref[...] + own * own * k0_ref[...]).astype(BF16)


def settle_kernel(shift_ref, k0_ref, k1_ref, k2_ref, s2_ref, rows1_ref, rows2_ref, moment_ref):
    width = moment_ref.shape[1]
    c = shift_ref[0:1, 0:1]
    k0, k1 = k0_ref[...], k1_ref[...]
    s1 = k1 - c * k0
    s2 = k2_ref[...] - 2 * c * k1 + c * c * k0
    s2_ref[...] = s2
    for at in range(0, k0.shape[1], width):
        rows1_ref[at : at + width, :] = s1[:, at : at + width].T
        rows2_ref[at : at + width, :] = s2[:, at : at + width].T
    for i, value in enumerate((k0 * s1, s1 * s1, s1 * s2, s2 * s2)):
        moment_ref[i : i + 1, :] = column_sums(value, width)


def cross_third_kernel(
    band_ref, ridge_ref, shift_ref, mean_ref, k_ref, local0_ref, local1_ref, local_ref,
    before0_ref, before1_ref, after0_ref, after1_ref, qn0_ref, qf0_ref,
    near_ref, far_ref, sum_ref, form_ref
):
    width = form_ref.shape[1]
    c = shift_ref[0:1, 0:1]
    own, mean_near, mean_far, mean_before, mean_after = (mean_ref[i : i + 1, 0:1] - c for i in range(5))
    before, after = neighbours(near_ref, far_ref, k_ref.shape[0])
    form = jnp.zeros((k_ref.shape[0], width), F32)

    def known(gap, zeroth_ref, first_ref, out):
        zeroth, first = zeroth_ref[:, out].astype(F32), first_ref[:, out].astype(F32)
        return 2 * gap * first + gap * gap * zeroth

    for j in range(0, band_ref.shape[0] // 3, 2):
        out, first, second = forward_products(band_ref, before, after, j)
        first = first + known(mean_before, before0_ref, before1_ref, out)
        second = second + known(mean_after, after0_ref, after1_ref, out)
        local = local_ref[:, out] + known(own, local0_ref, local1_ref, out)
        back = mean_near * mean_near * qn0_ref[: k_ref.shape[0], out].astype(F32)
        back = back + mean_far * mean_far * qf0_ref[: k_ref.shape[0], out].astype(F32)
        mine = (ridge_ref[:, out] - c) * k_ref[:, out] + 0.5 * local
        sum_ref[:, out] = mine + 0.5 * (first + second + back)
        part = k_ref[:, out] * (mine + first + second)
        form = form + part[:, :width] + part[:, width:]
    form_ref[...] = jnp.sum(form.T, axis=0, keepdims=True)


def finish_third_kernel(sum_ref, q_ref, rows3_ref):
    width = rows3_ref.shape[1]
    for at in range(0, sum_ref.shape[1], width):
        out = slice(at, at + width)
        rows3_ref[out, :] = (sum_ref[:, out] + 0.5 * q_ref[:, out].astype(F32)).T


def share(above, below):
    return jnp.where(below == 0, 0.0, above / below)


def scalars(m, shift, iters):
    zero = jnp.zeros_like(m[0])
    solution = [zero] * iters
    residual = [zero + 1.0] + [zero] * iters
    direction = [zero + 1.0] + [zero] * (iters - 1)

    def inner(a, b):
        total = zero
        for i, left in enumerate(a):
            for j, right in enumerate(b):
                if i + j < len(m):
                    total = total + left * right * m[i + j]
        return total

    now = m[0]
    for step in range(iters):
        used = direction[: step + 1]
        image = [shift * value for value in used] + [zero]
        for i, value in enumerate(used):
            image[i + 1] = image[i + 1] + value
        alpha = share(now, inner(used, image))
        for i, value in enumerate(used):
            solution[i] = solution[i] + alpha * value
        for i, value in enumerate(image):
            residual[i] = residual[i] - alpha * value
        if step + 1 < iters:
            left = residual[: step + 2]
            new = inner(left, left)
            beta = share(new, now)
            direction = [r + beta * d for r, d in zip(residual[:iters], direction, strict=True)]
            now = new
    return solution, residual


def combine_kernel(shift_ref, moment_ref, targets_ref, k1_ref, k2_ref, k3_ref, solution_ref, residual_ref):
    width = moment_ref.shape[1]
    m = [moment_ref[i : i + 1, :] for i in range(6)]
    x, r = scalars(m, shift_ref[...], 3)
    for at in range(0, targets_ref.shape[0], width):
        out = slice(at, at + width)
        k0 = targets_ref[out, :]
        k1, k2, k3 = k1_ref[out, :], k2_ref[out, :], k3_ref[out, :]
        solution_ref[out, :] = x[0] * k0 + x[1] * k1 + x[2] * k2
        residual_ref[out, :] = r[0] * k0 + r[1] * k1 + r[2] * k2 + r[3] * k3


def near(value):
    count = lax.axis_size("asset")
    return lax.ppermute(value, "asset", [(i, i ^ 1) for i in range(count)])


def far(value):
    count = lax.axis_size("asset")
    return lax.ppermute(
        value, "asset", [(i, (i + 1 if i % 2 else i - 1) % count) for i in range(count)]
    )


def forward(value):
    count = lax.axis_size("asset")
    return lax.ppermute(
        value, "asset", [(i, (i - 2 if i % 2 else i + 2) % count) for i in range(count)]
    )


def back(value):
    count = lax.axis_size("asset")
    return lax.ppermute(
        value, "asset", [(i, (i + 2 if i % 2 else i - 2) % count) for i in range(count)]
    )


def added(to_near, received):
    return (to_near.astype(F32) + received.astype(F32)).astype(BF16)


def sum_step(value, axis, distance):
    count = lax.axis_size(axis)
    return value + lax.ppermute(value, axis, [(i, i ^ distance) for i in range(count)])


def sum_over(value, axis):
    count = lax.axis_size(axis)
    step = 1
    while step < count:
        total = value
        for distance in (step, 2 * step, 3 * step) if 2 * step < count else (step,):
            route = [(i, i ^ distance) for i in range(count)]
            total = total + lax.ppermute(value, axis, route)
        value = total
        step *= 4
    return value


def together(*values):
    return lax.optimization_barrier(values)


def shards(targets, ridge, blocks, col_index, row_length):
    rows, slots, height, width = blocks.shape
    cols = targets.shape[1]
    assets = rows * width
    devices = lax.axis_size("asset")
    halves = lax.axis_size("rhs")
    ridge = ridge[None, :]

    def shape(kind, *dims):
        return jax.ShapeDtypeStruct(dims, kind)

    field, rounded, row = shape(F32, cols, assets), shape(BF16, cols, assets), shape(F32, 1, cols)
    band_shape = shape(BF16, 3 * rows + 1, assets, width)
    if halves == 2:
        part, other = blocks, lax.ppermute(blocks, "rhs", [(0, 1), (1, 0)])
    else:
        part, other = lax.all_gather(blocks, "rhs", axis=2, tiled=True), None

    k0, v0, m0 = call(prepare_kernel, (field, rounded, row), (targets,), flops=5 * 10**9)
    near0 = near(v0)
    band = call(spread_first_kernel, band_shape, (col_index, row_length, part), smem=2)
    if other is not None:
        band = call(
            spread_other_kernel, band_shape, (col_index, row_length, other, band), smem=2, aliases={3: 0}
        )
    distances = [1 << i for i in range(1, (devices - 1).bit_length())]
    pieces, message = (field,) * 3, shape(BF16, cols + 16, assets)

    to_near, to_far = call(products_first_kernel, (message,) * 2, (band, v0, ridge))
    qf0, qn0 = far(to_far), near(to_near)
    local0 = call(local_kernel, field, (band, together(v0, to_near)[0]))
    far0 = forward(together(near0, local0)[0])
    partial, means = call(
        gather_first_kernel, (field, shape(F32, 8, width)), (ridge, k0, local0, to_near, qn0, qf0)
    )
    k1, v1, before0, after0 = call(
        cross_first_kernel, (field, rounded, field, field), (band, partial, k0, means, near0, far0)
    )

    to_near1, to_far1 = call(products_kernel, (rounded,) * 2, (band, v1))
    received, near1 = back(to_far1), near(v1)
    far1 = forward(near1)
    mean = together(means[5:6], to_near1)[0]
    for distance in distances[:-2]:
        mean = sum_step(mean, "asset", distance)
    received, mean = together(received, mean)
    q1 = near(added(to_near1, received))
    local1 = call(local_kernel, field, (band, v1))
    for distance in distances[-2:-1]:
        mean = sum_step(mean, "asset", distance)
    partial, before1, after1 = call(
        cross_second_kernel,
        pieces,
        (band, ridge, means, k1, local0, local1, before0, after0, qn0, qf0, near1, far1),
    )
    mean, _ = together(mean, partial)
    shift = sum_step(mean, "asset", distances[-1]) / devices
    k2, v2 = call(finish_second_kernel, (field, rounded), (k0, k1, means, partial, q1))

    far2, near2 = far(v2), near(v2)
    to_near, to_far, _, _ = call(
        products_third_kernel, (rounded,) * 4, (band, shift, means, to_near1, to_far1, v2)
    )
    q2 = near(added(to_near, back(to_far)))
    local2 = call(local_kernel, field, (band, v2))
    out = shape(F32, assets, cols)
    s2, rows1, rows2, pairs = call(
        settle_kernel, (field, out, out, shape(F32, 4, cols)), (shift, k0, k1, k2)
    )
    partial, form = call(
        cross_third_kernel,
        (field, row),
        (
            band, ridge, shift, means, s2, local0, local1, local2, before0, before1, after0, after1,
            qn0, qf0, near2, far2,
        ),
    )
    moments = sum_over(jnp.concatenate([m0, pairs, form]), "asset")
    rows3 = call(finish_third_kernel, out, (partial, q2))
    return call(combine_kernel, (out, out), (shift, moments, targets, rows1, rows2, rows3))


def solution(mesh):
    return jax.shard_map(
        shards,
        mesh=mesh,
        in_specs=(
            P("asset", "rhs"),
            P("asset"),
            P("asset", None, "rhs", None),
            P("asset", None),
            P("asset"),
        ),
        out_specs=(P("asset", "rhs"), P("asset", "rhs")),
        check_vma=False,
    )
```

```python
import jax
import jax.numpy as jnp
from jax import lax
from jax.experimental import pallas as pl
from jax.experimental.pallas import tpu as pltpu
from jax.sharding import PartitionSpec as P

F32 = jnp.float32
BF16 = jnp.bfloat16
VMEM = pl.BlockSpec(memory_space=pltpu.VMEM)
SMEM = pl.BlockSpec(memory_space=pltpu.SMEM)
LIMIT = 8 * 1024 * 1024
HBM = pl.BlockSpec(memory_space=pltpu.HBM)
NN = (((1,), (0,)), ((), ()))
NT = (((1,), (1,)), ((), ()))


def call(kernel, out_shape, args, smem=0, outside=(), scratch=(), aliases=None, flops=0):
    specs = [SMEM] * smem + [VMEM] * (len(args) - smem)
    for at in outside:
        specs[at] = HBM
    return pl.pallas_call(
        kernel,
        out_shape=out_shape,
        in_specs=specs,
        out_specs=jax.tree.map(lambda _: VMEM, out_shape),
        scratch_shapes=scratch,
        input_output_aliases=aliases or {},
        cost_estimate=pl.CostEstimate(flops=flops, bytes_accessed=2**20, transcendentals=0) if flops else None,
        compiler_params=pltpu.CompilerParams(vmem_limit_bytes=LIMIT),
    )(*args)


def column_sums(values, width):
    folded = values[:, :width]
    for at in range(width, values.shape[1], width):
        folded = folded + values[:, at : at + width]
    return jnp.sum(folded.T, axis=0, keepdims=True)


def prepare_kernel(targets_ref, base_ref, rounded_ref, moment_ref):
    assets = targets_ref.shape[0]
    width = moment_ref.shape[1]
    for at in range(0, assets, width):
        tile = targets_ref[at : at + width, :].T
        base_ref[:, at : at + width] = tile
        rounded_ref[:, at : at + width] = tile.astype(BF16)
    values = targets_ref[...]
    moment_ref[...] = jnp.sum(values * values, axis=0, keepdims=True)


def place_blocks(col_ref, length_ref, offset, part_ref, band_ref):
    rows, slots, height, width = part_ref.shape
    spare = band_ref.shape[0] - 1
    total = rows * lax.axis_size("asset")
    first = lax.axis_index("asset") * rows - rows

    def one_row(row, carry):
        at = pl.ds(pl.multiple_of(row * width + offset, height), height)
        for slot in range(slots):
            place = col_ref[row, slot] - first
            place = jnp.where(place < 0, place + total, place)
            place = jnp.where(place >= total, place - total, place)
            place = jnp.where(slot < length_ref[row], place, spare)
            band_ref[place, at, :] = part_ref[row, slot]
        return carry

    lax.fori_loop(0, rows, one_row, 0)


def spread_first_kernel(col_ref, length_ref, part_ref, ridge_ref, band_ref, mean_ref):
    mean = jnp.sum(ridge_ref[...], axis=1, keepdims=True) / ridge_ref.shape[1]
    mean_ref[...] = jnp.broadcast_to(mean, mean_ref.shape)
    band_ref[...] = jnp.zeros_like(band_ref)
    height = part_ref.shape[2]
    mine = 0 if height == part_ref.shape[3] else lax.axis_index("rhs") * height
    place_blocks(col_ref, length_ref, mine, part_ref, band_ref)


def spread_other_kernel(col_ref, length_ref, part_ref, _, band_ref):
    height = part_ref.shape[2]
    place_blocks(col_ref, length_ref, (1 - lax.axis_index("rhs")) * height, part_ref, band_ref)


def is_odd(dims):
    return jnp.full(dims, lax.axis_index("asset") % 2, jnp.int32) == 1


def columns(ref, first, last, rows):
    return jnp.concatenate([ref[c, rows, :] for c in range(first, last)], axis=1)


def products_kernel(band_ref, v_ref, near_ref, far_ref):
    places, _, width = band_ref.shape
    rows = places // 3
    cols = v_ref.shape[0]
    odd = is_odd((cols, 2 * width))
    for j in range(0, rows, 2):
        out = slice(j * width, (j + 2) * width)
        low = slice(0, (j + 2) * width)
        high = slice(j * width, rows * width)
        before = lax.dot_general(
            v_ref[:, low], columns(band_ref, j, j + 2, low), NN, preferred_element_type=F32
        )
        after = lax.dot_general(
            v_ref[:, high],
            columns(band_ref, 2 * rows + j, 2 * rows + j + 2, high),
            NN,
            preferred_element_type=F32,
        )
        near_ref[:cols, out] = jnp.where(odd, before, after).astype(BF16)
        far_ref[:cols, out] = jnp.where(odd, after, before).astype(BF16)


def products_first_kernel(band_ref, v_ref, ridge_ref, near_ref, far_ref):
    products_kernel(band_ref, v_ref, near_ref, far_ref)
    cols, assets = v_ref.shape
    mean = jnp.sum(ridge_ref[...], axis=1, keepdims=True) / assets
    rest = jnp.broadcast_to(mean, (near_ref.shape[0] - cols, assets)).astype(BF16)
    near_ref[cols:, :] = rest
    far_ref[cols:, :] = rest


def products_second_kernel(band_ref, v_ref, mean_ref, near_ref, far_ref):
    products_kernel(band_ref, v_ref, near_ref, far_ref)
    cols = v_ref.shape[0]
    rest = (far_ref.shape[0] - cols, far_ref.shape[1])
    far_ref[cols:, :] = jnp.broadcast_to(mean_ref[0:1, 0:1], rest).astype(BF16)


def local_kernel(band_ref, v_ref, out_ref):
    places, _, width = band_ref.shape
    rows = places // 3
    cols = out_ref.shape[0]
    every = slice(0, rows * width)
    for j in range(0, rows, 2):
        out = slice(j * width, (j + 2) * width)
        out_ref[:, out] = lax.dot_general(
            v_ref[:cols, :],
            columns(band_ref, rows + j, rows + j + 2, every),
            NN,
            preferred_element_type=F32,
        ) + lax.dot_general(
            v_ref[:cols, :], columns(band_ref, rows, 2 * rows, out), NT, preferred_element_type=F32
        )


def neighbours(near_ref, far_ref, cols):
    near, far = near_ref[:cols, :].astype(F32), far_ref[:cols, :].astype(F32)
    odd = is_odd(near.shape)
    return jnp.where(odd, near, far).astype(BF16), jnp.where(odd, far, near).astype(BF16)


def forward_products(band_ref, before, after, j):
    places, _, width = band_ref.shape
    rows = places // 3
    out = slice(j * width, (j + 2) * width)
    return out, lax.dot_general(
        before[:, j * width :], columns(band_ref, j, rows, out), NT, preferred_element_type=F32
    ), lax.dot_general(
        after[:, : (j + 2) * width],
        columns(band_ref, 2 * rows, 2 * rows + j + 2, out),
        NT,
        preferred_element_type=F32,
    )


def gather_first_kernel(ridge_ref, k_ref, local_ref, own_ref, near_ref, far_ref, sum_ref, mean_ref):
    cols, width = k_ref.shape[0], mean_ref.shape[1]
    means = [ref[cols : cols + 8, :width].astype(F32)[:1] for ref in (own_ref, near_ref, far_ref)]
    odd = is_odd(means[0].shape)
    means += [jnp.where(odd, means[1], means[2]), jnp.where(odd, means[2], means[1])]
    means.append(means[0] + means[1])
    for i, value in enumerate(means):
        mean_ref[i : i + 1, :] = value
    both = local_ref[...] + near_ref[:cols, :].astype(F32) + far_ref[:cols, :].astype(F32)
    sum_ref[...] = ridge_ref[...] * k_ref[...] + 0.5 * both


def cross_first_kernel(
    band_ref, sum_ref, k_ref, mean_ref, near_ref, far_ref, next_ref, rounded_ref, before_ref, after_ref
):
    before, after = neighbours(near_ref, far_ref, k_ref.shape[0])
    for j in range(0, band_ref.shape[0] // 3, 2):
        out, first, second = forward_products(band_ref, before, after, j)
        before_ref[:, out] = first
        after_ref[:, out] = second
        value = sum_ref[:, out] + 0.5 * (first + second)
        next_ref[:, out] = value
        rounded_ref[:, out] = (value - mean_ref[0:1, 0:1] * k_ref[:, out]).astype(BF16)


def cross_second_kernel(
    band_ref, ridge_ref, mean_ref, k_ref, local0_ref, local_ref, before0_ref, after0_ref, qn0_ref, qf0_ref,
    near_ref, far_ref, sum_ref, before_ref, after_ref
):
    own, mean_near, mean_far, mean_before, mean_after = (mean_ref[i : i + 1, 0:1] for i in range(5))
    before, after = neighbours(near_ref, far_ref, k_ref.shape[0])
    for j in range(0, band_ref.shape[0] // 3, 2):
        out, first, second = forward_products(band_ref, before, after, j)
        before_ref[:, out] = first
        after_ref[:, out] = second
        known = own * local0_ref[:, out] + mean_before * before0_ref[:, out] + mean_after * after0_ref[:, out]
        known = known + mean_near * qn0_ref[: k_ref.shape[0], out].astype(F32) + mean_far * qf0_ref[: k_ref.shape[0], out].astype(F32)
        both = local_ref[:, out] + first + second + known
        sum_ref[:, out] = ridge_ref[:, out] * k_ref[:, out] + 0.5 * both


def finish_second_kernel(
    k0_ref, k_ref, mean_ref, sum_ref, own_ref, q_ref, next_ref, rounded_ref, total_ref
):
    cols, width = k_ref.shape[0], total_ref.shape[1]
    sums = [ref[cols : cols + 8, :width].astype(F32)[:1] for ref in (own_ref, q_ref)]
    total_ref[...] = sums[0] + sums[1]
    value = sum_ref[...] + 0.5 * q_ref[:cols, :].astype(F32)
    next_ref[...] = value
    own = mean_ref[0:1, 0:1]
    rounded_ref[...] = (value - 2 * own * k_ref[...] + own * own * k0_ref[...]).astype(BF16)


def settle_kernel(
    shift_ref, mean_ref, ridge_ref, k0_ref, k1_ref, k2_ref, local0_ref, local1_ref, local2_ref,
    before0_ref, before1_ref, after0_ref, after1_ref, qn0_ref, qf0_ref,
    sum_ref, rows1_ref, rows2_ref, moment_ref
):
    cols, width = k0_ref.shape[0], moment_ref.shape[1]
    c = shift_ref[0:1, 0:1]
    own, mean_near, mean_far, mean_before, mean_after = (mean_ref[i : i + 1, 0:1] - c for i in range(5))
    totals = [jnp.zeros((cols, width), F32)] * 5
    for at in range(0, k0_ref.shape[1], width):
        out = slice(at, at + width)
        k0, k1 = k0_ref[:, out], k1_ref[:, out]
        s1 = k1 - c * k0
        s2 = k2_ref[:, out] - 2 * c * k1 + c * c * k0
        rows1_ref[out, :] = s1.T
        rows2_ref[out, :] = s2.T
        local = local2_ref[:, out] + 2 * own * local1_ref[:, out] + own * own * local0_ref[:, out]
        mine = (ridge_ref[:, out] - c) * s2 + 0.5 * local
        known = 2 * mean_before * before1_ref[:, out] + mean_before * mean_before * before0_ref[:, out]
        known = known + 2 * mean_after * after1_ref[:, out] + mean_after * mean_after * after0_ref[:, out]
        back = mean_near * mean_near * qn0_ref[:cols, out].astype(F32)
        back = back + mean_far * mean_far * qf0_ref[:cols, out].astype(F32)
        sum_ref[:, out] = mine + 0.5 * (known + back)
        parts = (k0 * s1, s1 * s1, s1 * s2, s2 * s2, s2 * (mine + back))
        totals = [total + part for total, part in zip(totals, parts, strict=True)]
    for i, total in enumerate(totals):
        moment_ref[i : i + 1, :] = jnp.sum(total.T, axis=0, keepdims=True)


def form_kernel(
    shift_ref, mean_ref, m0_ref, pairs_ref, to2_ref, to1_ref, r2_ref, r1_ref, near2_ref, near1_ref, near0_ref,
    q_ref, moment_ref
):
    cols, assets = to2_ref.shape
    width = moment_ref.shape[1]
    c = shift_ref[0:1, 0:1]
    own, gap = mean_ref[0:1, 0:1] - c, mean_ref[1:2, 0:1] - c
    other = r1_ref[cols : cols + 8, :width].astype(F32)[:1, :1] - c
    total = jnp.zeros((cols, width), F32)
    for at in range(0, assets, width):
        out = slice(at, at + width)
        both = to2_ref[:, out].astype(F32) + 2 * own * to1_ref[:, out].astype(F32)
        both = both + r2_ref[:, out].astype(F32) + 2 * other * r1_ref[:cols, out].astype(F32)
        field = near2_ref[:, out].astype(F32) + 2 * gap * near1_ref[:, out].astype(F32)
        field = field + gap * gap * near0_ref[:, out].astype(F32)
        q_ref[:, out] = both.astype(BF16)
        total = total + both * field
    moment_ref[0:1, :] = m0_ref[...]
    moment_ref[1:5, :] = pairs_ref[0:4, :]
    moment_ref[5:6, :] = pairs_ref[4:5, :] + jnp.sum(total.T, axis=0, keepdims=True)
    moment_ref[6:8, :] = jnp.zeros((2, width), F32)


def cross_third_kernel(band_ref, known_ref, near_ref, far_ref, sum_ref):
    before, after = neighbours(near_ref, far_ref, known_ref.shape[0])
    for j in range(0, band_ref.shape[0] // 3, 2):
        out, first, second = forward_products(band_ref, before, after, j)
        sum_ref[:, out] = known_ref[:, out] + 0.5 * (first + second)


def finish_third_kernel(sum_ref, q_ref, rows3_ref):
    width = rows3_ref.shape[1]
    for at in range(0, sum_ref.shape[1], width):
        out = slice(at, at + width)
        rows3_ref[out, :] = (sum_ref[:, out] + 0.5 * q_ref[:, out].astype(F32)).T


def share(above, below):
    return jnp.where(below == 0, 0.0, above / below)


def scalars(m, shift, iters):
    zero = jnp.zeros_like(m[0])
    solution = [zero] * iters
    residual = [zero + 1.0] + [zero] * iters
    direction = [zero + 1.0] + [zero] * (iters - 1)

    def inner(a, b):
        total = zero
        for i, left in enumerate(a):
            for j, right in enumerate(b):
                if i + j < len(m):
                    total = total + left * right * m[i + j]
        return total

    now = m[0]
    for step in range(iters):
        used = direction[: step + 1]
        image = [shift * value for value in used] + [zero]
        for i, value in enumerate(used):
            image[i + 1] = image[i + 1] + value
        alpha = share(now, inner(used, image))
        for i, value in enumerate(used):
            solution[i] = solution[i] + alpha * value
        for i, value in enumerate(image):
            residual[i] = residual[i] - alpha * value
        if step + 1 < iters:
            left = residual[: step + 2]
            new = inner(left, left)
            beta = share(new, now)
            direction = [r + beta * d for r, d in zip(residual[:iters], direction, strict=True)]
            now = new
    return solution, residual


def combine_kernel(shift_ref, moment_ref, targets_ref, k1_ref, k2_ref, k3_ref, solution_ref, residual_ref):
    width = moment_ref.shape[1]
    m = [moment_ref[i : i + 1, :] for i in range(6)]
    x, r = scalars(m, shift_ref[...], 3)
    for at in range(0, targets_ref.shape[0], width):
        out = slice(at, at + width)
        k0 = targets_ref[out, :]
        k1, k2, k3 = k1_ref[out, :], k2_ref[out, :], k3_ref[out, :]
        solution_ref[out, :] = x[0] * k0 + x[1] * k1 + x[2] * k2
        residual_ref[out, :] = r[0] * k0 + r[1] * k1 + r[2] * k2 + r[3] * k3


def near(value):
    count = lax.axis_size("asset")
    return lax.ppermute(value, "asset", [(i, i ^ 1) for i in range(count)])


def far(value):
    count = lax.axis_size("asset")
    return lax.ppermute(
        value, "asset", [(i, (i + 1 if i % 2 else i - 1) % count) for i in range(count)]
    )


def forward(value):
    count = lax.axis_size("asset")
    return lax.ppermute(
        value, "asset", [(i, (i - 2 if i % 2 else i + 2) % count) for i in range(count)]
    )


def back(value):
    count = lax.axis_size("asset")
    return lax.ppermute(
        value, "asset", [(i, (i + 2 if i % 2 else i - 2) % count) for i in range(count)]
    )


def add_kernel(near_ref, received_ref, mean_ref, out_ref):
    cols = near_ref.shape[0]
    out_ref[:cols, :] = (near_ref[...].astype(F32) + received_ref[:cols, :].astype(F32)).astype(BF16)
    rest = (out_ref.shape[0] - cols, out_ref.shape[1])
    out_ref[cols:, :] = jnp.broadcast_to(mean_ref[0:1, 0:1], rest).astype(BF16)


def sum_step(value, axis, distance):
    count = lax.axis_size(axis)
    return value + lax.ppermute(value, axis, [(i, i ^ distance) for i in range(count)])


def sum_four(value, axis, first, second):
    count = lax.axis_size(axis)
    total = value
    for distance in (first, second, first + second):
        total = total + lax.ppermute(value, axis, [(i, i ^ distance) for i in range(count)])
    return total


def sum_over(value, axis):
    count = lax.axis_size(axis)
    step = 1
    while step < count:
        total = value
        for distance in (step, 2 * step, 3 * step) if 2 * step < count else (step,):
            route = [(i, i ^ distance) for i in range(count)]
            total = total + lax.ppermute(value, axis, route)
        value = total
        step *= 4
    return value


def together(*values):
    return lax.optimization_barrier(values)


def shards(targets, ridge, blocks, col_index, row_length):
    rows, slots, height, width = blocks.shape
    cols = targets.shape[1]
    assets = rows * width
    devices = lax.axis_size("asset")
    halves = lax.axis_size("rhs")
    ridge = ridge[None, :]

    def shape(kind, *dims):
        return jax.ShapeDtypeStruct(dims, kind)

    field, rounded, row = shape(F32, cols, assets), shape(BF16, cols, assets), shape(F32, 1, cols)
    band_shape = shape(BF16, 3 * rows + 1, assets, width)
    if halves == 2:
        part, other = blocks, lax.ppermute(blocks, "rhs", [(0, 1), (1, 0)])
    else:
        part, other = lax.all_gather(blocks, "rhs", axis=2, tiled=True), None

    k0, v0, m0 = call(prepare_kernel, (field, rounded, row), (targets,), flops=5 * 10**9)
    near0 = near(v0)
    band, mean = call(
        spread_first_kernel,
        (band_shape, shape(F32, 1, width)),
        (col_index, row_length, part, ridge),
        smem=2,
    )
    if other is not None:
        band = call(
            spread_other_kernel, band_shape, (col_index, row_length, other, band), smem=2, aliases={3: 0}
        )
    distances = [1 << i for i in range(1, (devices - 1).bit_length())]
    pieces, message = (field,) * 3, shape(BF16, cols + 16, assets)

    to_near, to_far = call(products_first_kernel, (message,) * 2, (band, v0, ridge))
    qf0, qn0 = far(to_far), near(to_near)
    local0 = call(local_kernel, field, (band, together(v0, to_near)[0]))
    far0 = forward(together(near0, local0)[0])
    mean = together(mean, local0)[0]
    for distance in distances[1:-1]:
        mean = sum_step(mean, "asset", distance)
    mean, local0 = together(mean, local0)
    partial, means = call(
        gather_first_kernel, (field, shape(F32, 8, width)), (ridge, k0, local0, to_near, qn0, qf0)
    )
    k1, v1, before0, after0 = call(
        cross_first_kernel, (field, rounded, field, field), (band, partial, k0, means, near0, far0)
    )

    to_near1, to_far1 = call(products_second_kernel, (rounded, message), (band, v1, means))
    received, near1 = back(to_far1), near(v1)
    far1 = forward(near1)
    mean = sum_four(together(mean, to_near1)[0], "asset", distances[0], distances[-1])
    joined = call(add_kernel, message, (to_near1, received, mean))
    q1 = near(joined)
    local1 = call(local_kernel, field, (band, v1))
    partial, before1, after1 = call(
        cross_second_kernel,
        pieces,
        (band, ridge, means, k1, local0, local1, before0, after0, qn0, qf0, near1, far1),
    )
    k2, v2, mean = call(
        finish_second_kernel,
        (field, rounded, shape(F32, 1, width)),
        (k0, k1, means, partial, joined, q1),
    )

    to_near2, to_far2 = call(products_kernel, (rounded,) * 2, (band, v2))
    near2 = near(together(v2, to_near2)[0])
    far2 = forward(near2)
    received2 = back(to_far2)
    local2 = call(local_kernel, field, (band, v2))
    shift = mean / devices
    out = shape(F32, assets, cols)
    known, rows1, rows2, pairs = call(
        settle_kernel,
        (field, out, out, shape(F32, 8, cols)),
        (
            shift, means, ridge, k0, k1, k2, local0, local1, local2,
            before0, before1, after0, after1, qn0, qf0,
        ),
    )
    joined, moments = call(
        form_kernel,
        (rounded, shape(F32, 8, cols)),
        (shift, means, m0, pairs, to_near2, to_near1, received2, received, near2, near1, near0),
    )
    moments = sum_over(moments, "asset")
    q2 = near(joined)
    partial = call(cross_third_kernel, field, (band, known, near2, far2))
    rows3 = call(finish_third_kernel, out, (partial, q2))
    return call(combine_kernel, (out, out), (shift, moments, targets, rows1, rows2, rows3))


def solution(mesh):
    return jax.shard_map(
        shards,
        mesh=mesh,
        in_specs=(
            P("asset", "rhs"),
            P("asset"),
            P("asset", None, "rhs", None),
            P("asset", None),
            P("asset"),
        ),
        out_specs=(P("asset", "rhs"), P("asset", "rhs")),
        check_vma=False,
    )
```

```python
import jax
import jax.numpy as jnp
from jax import lax
from jax.experimental import pallas as pl
from jax.experimental.pallas import tpu as pltpu
from jax.sharding import PartitionSpec as P

F32 = jnp.float32
BF16 = jnp.bfloat16
VMEM = pl.BlockSpec(memory_space=pltpu.VMEM)
SMEM = pl.BlockSpec(memory_space=pltpu.SMEM)
LIMIT = 8 * 1024 * 1024
HBM = pl.BlockSpec(memory_space=pltpu.HBM)
NN = (((1,), (0,)), ((), ()))
NT = (((1,), (1,)), ((), ()))


def call(kernel, out_shape, args, smem=0, outside=(), scratch=(), aliases=None, flops=0, results=VMEM):
    specs = [SMEM] * smem + [VMEM] * (len(args) - smem)
    for at in outside:
        specs[at] = HBM
    return pl.pallas_call(
        kernel,
        out_shape=out_shape,
        in_specs=specs,
        out_specs=jax.tree.map(lambda _: results, out_shape),
        scratch_shapes=scratch,
        input_output_aliases=aliases or {},
        cost_estimate=pl.CostEstimate(flops=flops, bytes_accessed=2**20, transcendentals=0) if flops else None,
        compiler_params=pltpu.CompilerParams(vmem_limit_bytes=LIMIT),
    )(*args)


def column_sums(values, width):
    folded = values[:, :width]
    for at in range(width, values.shape[1], width):
        folded = folded + values[:, at : at + width]
    return jnp.sum(folded.T, axis=0, keepdims=True)


def prepare_kernel(targets_ref, base_ref, rounded_ref, moment_ref):
    assets = targets_ref.shape[0]
    width = moment_ref.shape[1]
    for at in range(0, assets, width):
        tile = targets_ref[at : at + width, :].T
        base_ref[:, at : at + width] = tile
        rounded_ref[:, at : at + width] = tile.astype(BF16)
    values = targets_ref[...]
    moment_ref[...] = jnp.sum(values * values, axis=0, keepdims=True)


def place_blocks(col_ref, length_ref, offset, part_ref, band_ref):
    rows, slots, height, width = part_ref.shape
    spare = band_ref.shape[0] - 1
    total = rows * lax.axis_size("asset")
    first = lax.axis_index("asset") * rows - rows

    def one_row(row, carry):
        at = pl.ds(pl.multiple_of(row * width + offset, height), height)
        for slot in range(slots):
            place = col_ref[row, slot] - first
            place = jnp.where(place < 0, place + total, place)
            place = jnp.where(place >= total, place - total, place)
            place = jnp.where(slot < length_ref[row], place, spare)
            band_ref[place, at, :] = part_ref[row, slot]
        return carry

    lax.fori_loop(0, rows, one_row, 0)


def spread_first_kernel(col_ref, length_ref, part_ref, ridge_ref, band_ref, mean_ref):
    mean = jnp.sum(ridge_ref[...], axis=1, keepdims=True) / ridge_ref.shape[1]
    mean_ref[...] = jnp.broadcast_to(mean, mean_ref.shape)
    band_ref[...] = jnp.zeros_like(band_ref)
    height = part_ref.shape[2]
    mine = 0 if height == part_ref.shape[3] else lax.axis_index("rhs") * height
    place_blocks(col_ref, length_ref, mine, part_ref, band_ref)


def spread_other_kernel(col_ref, length_ref, part_ref, _, band_ref):
    height = part_ref.shape[2]
    place_blocks(col_ref, length_ref, (1 - lax.axis_index("rhs")) * height, part_ref, band_ref)


def is_odd(dims):
    return jnp.full(dims, lax.axis_index("asset") % 2, jnp.int32) == 1


def columns(ref, first, last, rows):
    return jnp.concatenate([ref[c, rows, :] for c in range(first, last)], axis=1)


def products_kernel(band_ref, v_ref, near_ref, far_ref):
    places, _, width = band_ref.shape
    rows = places // 3
    cols = v_ref.shape[0]
    odd = is_odd((cols, 2 * width))
    for j in range(0, rows, 2):
        out = slice(j * width, (j + 2) * width)
        low = slice(0, (j + 2) * width)
        high = slice(j * width, rows * width)
        before = lax.dot_general(
            v_ref[:, low], columns(band_ref, j, j + 2, low), NN, preferred_element_type=F32
        )
        after = lax.dot_general(
            v_ref[:, high],
            columns(band_ref, 2 * rows + j, 2 * rows + j + 2, high),
            NN,
            preferred_element_type=F32,
        )
        near_ref[:cols, out] = jnp.where(odd, before, after).astype(BF16)
        far_ref[:cols, out] = jnp.where(odd, after, before).astype(BF16)


def products_first_kernel(band_ref, v_ref, ridge_ref, near_ref, far_ref):
    products_kernel(band_ref, v_ref, near_ref, far_ref)
    cols, assets = v_ref.shape
    mean = jnp.sum(ridge_ref[...], axis=1, keepdims=True) / assets
    rest = jnp.broadcast_to(mean, (near_ref.shape[0] - cols, assets)).astype(BF16)
    near_ref[cols:, :] = rest
    far_ref[cols:, :] = rest


def products_second_kernel(band_ref, v_ref, mean_ref, near_ref, far_ref):
    products_kernel(band_ref, v_ref, near_ref, far_ref)
    cols = v_ref.shape[0]
    rest = (far_ref.shape[0] - cols, far_ref.shape[1])
    far_ref[cols:, :] = jnp.broadcast_to(mean_ref[0:1, 0:1], rest).astype(BF16)


def local_kernel(band_ref, v_ref, out_ref):
    places, _, width = band_ref.shape
    rows = places // 3
    cols = out_ref.shape[0]
    every = slice(0, rows * width)
    for j in range(0, rows, 2):
        out = slice(j * width, (j + 2) * width)
        out_ref[:, out] = lax.dot_general(
            v_ref[:cols, :],
            columns(band_ref, rows + j, rows + j + 2, every),
            NN,
            preferred_element_type=F32,
        ) + lax.dot_general(
            v_ref[:cols, :], columns(band_ref, rows, 2 * rows, out), NT, preferred_element_type=F32
        )


def neighbours(near_ref, far_ref, cols):
    near, far = near_ref[:cols, :].astype(F32), far_ref[:cols, :].astype(F32)
    odd = is_odd(near.shape)
    return jnp.where(odd, near, far).astype(BF16), jnp.where(odd, far, near).astype(BF16)


def forward_products(band_ref, before, after, j):
    places, _, width = band_ref.shape
    rows = places // 3
    out = slice(j * width, (j + 2) * width)
    return out, lax.dot_general(
        before[:, j * width :], columns(band_ref, j, rows, out), NT, preferred_element_type=F32
    ), lax.dot_general(
        after[:, : (j + 2) * width],
        columns(band_ref, 2 * rows, 2 * rows + j + 2, out),
        NT,
        preferred_element_type=F32,
    )


def gather_first_kernel(ridge_ref, k_ref, local_ref, own_ref, near_ref, far_ref, sum_ref, mean_ref):
    cols, width = k_ref.shape[0], mean_ref.shape[1]
    means = [ref[cols : cols + 8, :width].astype(F32)[:1] for ref in (own_ref, near_ref, far_ref)]
    odd = is_odd(means[0].shape)
    means += [jnp.where(odd, means[1], means[2]), jnp.where(odd, means[2], means[1])]
    means.append(means[0] + means[1])
    for i, value in enumerate(means):
        mean_ref[i : i + 1, :] = value
    both = local_ref[...] + near_ref[:cols, :].astype(F32) + far_ref[:cols, :].astype(F32)
    sum_ref[...] = ridge_ref[...] * k_ref[...] + 0.5 * both


def cross_first_kernel(
    band_ref, sum_ref, k_ref, mean_ref, near_ref, far_ref, next_ref, rounded_ref, before_ref, after_ref
):
    before, after = neighbours(near_ref, far_ref, k_ref.shape[0])
    for j in range(0, band_ref.shape[0] // 3, 2):
        out, first, second = forward_products(band_ref, before, after, j)
        before_ref[:, out] = first
        after_ref[:, out] = second
        value = sum_ref[:, out] + 0.5 * (first + second)
        next_ref[:, out] = value
        rounded_ref[:, out] = (value - mean_ref[0:1, 0:1] * k_ref[:, out]).astype(BF16)


def cross_second_kernel(
    band_ref, ridge_ref, mean_ref, k_ref, local0_ref, local_ref, before0_ref, after0_ref, qn0_ref, qf0_ref,
    near_ref, far_ref, sum_ref, before_ref, after_ref
):
    own, mean_near, mean_far, mean_before, mean_after = (mean_ref[i : i + 1, 0:1] for i in range(5))
    before, after = neighbours(near_ref, far_ref, k_ref.shape[0])
    for j in range(0, band_ref.shape[0] // 3, 2):
        out, first, second = forward_products(band_ref, before, after, j)
        before_ref[:, out] = first
        after_ref[:, out] = second
        known = own * local0_ref[:, out] + mean_before * before0_ref[:, out] + mean_after * after0_ref[:, out]
        known = known + mean_near * qn0_ref[: k_ref.shape[0], out].astype(F32) + mean_far * qf0_ref[: k_ref.shape[0], out].astype(F32)
        both = local_ref[:, out] + first + second + known
        sum_ref[:, out] = ridge_ref[:, out] * k_ref[:, out] + 0.5 * both


def finish_second_kernel(
    k0_ref, k_ref, mean_ref, sum_ref, own_ref, q_ref, next_ref, rounded_ref, total_ref
):
    cols, width = k_ref.shape[0], total_ref.shape[1]
    sums = [ref[cols : cols + 8, :width].astype(F32)[:1] for ref in (own_ref, q_ref)]
    total_ref[...] = sums[0] + sums[1]
    value = sum_ref[...] + 0.5 * q_ref[:cols, :].astype(F32)
    next_ref[...] = value
    own = mean_ref[0:1, 0:1]
    rounded_ref[...] = (value - 2 * own * k_ref[...] + own * own * k0_ref[...]).astype(BF16)


def settle_kernel(
    shift_ref, mean_ref, ridge_ref, k0_ref, k1_ref, k2_ref, local0_ref, local1_ref, local2_ref,
    before0_ref, before1_ref, after0_ref, after1_ref, qn0_ref, qf0_ref,
    m0_ref, to2_ref, to1_ref, r1_ref, near1_ref, near0_ref,
    sum_ref, rows1_ref, rows2_ref, moment_ref, both_ref, field_ref
):
    cols, width = k0_ref.shape[0], moment_ref.shape[1]
    c = shift_ref[0:1, 0:1]
    own, mean_near, mean_far, mean_before, mean_after = (mean_ref[i : i + 1, 0:1] - c for i in range(5))
    other = r1_ref[cols : cols + 8, :width].astype(F32)[:1, :1] - c
    totals = [jnp.zeros((cols, width), F32)] * 5
    for at in range(0, k0_ref.shape[1], width):
        out = slice(at, at + width)
        k0, k1 = k0_ref[:, out], k1_ref[:, out]
        s1 = k1 - c * k0
        s2 = k2_ref[:, out] - 2 * c * k1 + c * c * k0
        rows1_ref[out, :] = s1.T
        rows2_ref[out, :] = s2.T
        local = local2_ref[:, out] + 2 * own * local1_ref[:, out] + own * own * local0_ref[:, out]
        mine = (ridge_ref[:, out] - c) * s2 + 0.5 * local
        known = 2 * mean_before * before1_ref[:, out] + mean_before * mean_before * before0_ref[:, out]
        known = known + 2 * mean_after * after1_ref[:, out] + mean_after * mean_after * after0_ref[:, out]
        back = mean_near * mean_near * qn0_ref[:cols, out].astype(F32)
        back = back + mean_far * mean_far * qf0_ref[:cols, out].astype(F32)
        sum_ref[:, out] = mine + 0.5 * (known + back)
        both = to2_ref[:, out].astype(F32) + 2 * own * to1_ref[:, out].astype(F32)
        both_ref[:, out] = both + 2 * other * r1_ref[:cols, out].astype(F32)
        field = 2 * mean_near * near1_ref[:, out].astype(F32)
        field_ref[:, out] = field + mean_near * mean_near * near0_ref[:, out].astype(F32)
        parts = (k0 * s1, s1 * s1, s1 * s2, s2 * s2, s2 * (mine + back))
        totals = [total + part for total, part in zip(totals, parts, strict=True)]
    moment_ref[0:1, :] = m0_ref[...]
    for i, total in enumerate(totals):
        moment_ref[i + 1 : i + 2, :] = jnp.sum(total.T, axis=0, keepdims=True)
    moment_ref[6:8, :] = jnp.zeros((2, width), F32)


def form_kernel(share_ref, both_ref, field_ref, received_ref, near_ref, q_ref, moment_ref):
    cols, assets = both_ref.shape
    width = moment_ref.shape[1]
    total = jnp.zeros((cols, width), F32)
    for at in range(0, assets, width):
        out = slice(at, at + width)
        both = both_ref[:, out] + received_ref[:, out].astype(F32)
        q_ref[:, out] = both.astype(BF16)
        total = total + both * (field_ref[:, out] + near_ref[:, out].astype(F32))
    moment_ref[...] = share_ref[...]
    moment_ref[5:6, :] = share_ref[5:6, :] + jnp.sum(total.T, axis=0, keepdims=True)


def cross_third_kernel(band_ref, known_ref, near_ref, far_ref, sum_ref):
    before, after = neighbours(near_ref, far_ref, known_ref.shape[0])
    for j in range(0, band_ref.shape[0] // 3, 2):
        out, first, second = forward_products(band_ref, before, after, j)
        sum_ref[:, out] = known_ref[:, out] + 0.5 * (first + second)


def finish_third_kernel(sum_ref, q_ref, rows3_ref):
    width = rows3_ref.shape[1]
    for at in range(0, sum_ref.shape[1], width):
        out = slice(at, at + width)
        rows3_ref[out, :] = (sum_ref[:, out] + 0.5 * q_ref[:, out].astype(F32)).T


def ratio(above, below):
    return jnp.where(below == 0, 0.0, above / below)


def scalars(m, shift, iters):
    zero = jnp.zeros_like(m[0])
    solution = [zero] * iters
    residual = [zero + 1.0] + [zero] * iters
    direction = [zero + 1.0] + [zero] * (iters - 1)

    def inner(a, b):
        total = zero
        for i, left in enumerate(a):
            for j, right in enumerate(b):
                if i + j < len(m):
                    total = total + left * right * m[i + j]
        return total

    now = m[0]
    for step in range(iters):
        used = direction[: step + 1]
        image = [shift * value for value in used] + [zero]
        for i, value in enumerate(used):
            image[i + 1] = image[i + 1] + value
        alpha = ratio(now, inner(used, image))
        for i, value in enumerate(used):
            solution[i] = solution[i] + alpha * value
        for i, value in enumerate(image):
            residual[i] = residual[i] - alpha * value
        if step + 1 < iters:
            left = residual[: step + 2]
            new = inner(left, left)
            beta = ratio(new, now)
            direction = [r + beta * d for r, d in zip(residual[:iters], direction, strict=True)]
            now = new
    return solution, residual


def combine_kernel(
    shift_ref, moment_ref, targets_ref, k1_ref, k2_ref, k3_ref, solution_hbm, residual_hbm, held, sems
):
    width = moment_ref.shape[1]
    m = [moment_ref[i : i + 1, :] for i in range(6)]
    x, r = scalars(m, shift_ref[...], 3)
    assets = targets_ref.shape[0]
    size = 2 * width
    copies = []
    for part in range(assets // size):
        out = slice(part * size, (part + 1) * size)
        k0, k1, k2, k3 = targets_ref[out, :], k1_ref[out, :], k2_ref[out, :], k3_ref[out, :]
        held[0, out, :] = x[0] * k0 + x[1] * k1 + x[2] * k2
        held[1, out, :] = r[0] * k0 + r[1] * k1 + r[2] * k2 + r[3] * k3
        for i, target in enumerate((solution_hbm, residual_hbm)):
            copy = pltpu.make_async_copy(held.at[i, out, :], target.at[out, :], sems.at[i, part])
            copy.start()
            copies.append(copy)
    for copy in copies:
        copy.wait()


def near(value):
    count = lax.axis_size("asset")
    return lax.ppermute(value, "asset", [(i, i ^ 1) for i in range(count)])


def far(value):
    count = lax.axis_size("asset")
    return lax.ppermute(
        value, "asset", [(i, (i + 1 if i % 2 else i - 1) % count) for i in range(count)]
    )


def forward(value):
    count = lax.axis_size("asset")
    return lax.ppermute(
        value, "asset", [(i, (i - 2 if i % 2 else i + 2) % count) for i in range(count)]
    )


def back(value):
    count = lax.axis_size("asset")
    return lax.ppermute(
        value, "asset", [(i, (i + 2 if i % 2 else i - 2) % count) for i in range(count)]
    )


def add_kernel(near_ref, received_ref, mean_ref, out_ref):
    cols = near_ref.shape[0]
    out_ref[:cols, :] = (near_ref[...].astype(F32) + received_ref[:cols, :].astype(F32)).astype(BF16)
    rest = (out_ref.shape[0] - cols, out_ref.shape[1])
    out_ref[cols:, :] = jnp.broadcast_to(mean_ref[0:1, 0:1], rest).astype(BF16)


def sum_step(value, axis, distance):
    count = lax.axis_size(axis)
    return value + lax.ppermute(value, axis, [(i, i ^ distance) for i in range(count)])


def sum_over(value, axis):
    count = lax.axis_size(axis)
    step = 1
    while step < count:
        total = value
        for distance in (step, 2 * step, 3 * step) if 2 * step < count else (step,):
            route = [(i, i ^ distance) for i in range(count)]
            total = total + lax.ppermute(value, axis, route)
        value = total
        step *= 4
    return value


def together(*values):
    return lax.optimization_barrier(values)


def shards(targets, ridge, blocks, col_index, row_length):
    rows, slots, height, width = blocks.shape
    cols = targets.shape[1]
    assets = rows * width
    devices = lax.axis_size("asset")
    halves = lax.axis_size("rhs")
    ridge = ridge[None, :]

    def shape(kind, *dims):
        return jax.ShapeDtypeStruct(dims, kind)

    field, rounded, row = shape(F32, cols, assets), shape(BF16, cols, assets), shape(F32, 1, cols)
    band_shape = shape(BF16, 3 * rows + 1, assets, width)
    if halves == 2:
        part, other = blocks, lax.ppermute(blocks, "rhs", [(0, 1), (1, 0)])
    else:
        part, other = lax.all_gather(blocks, "rhs", axis=2, tiled=True), None

    k0, v0, m0 = call(prepare_kernel, (field, rounded, row), (targets,), flops=5 * 10**9)
    near0 = near(v0)
    band, mean = call(
        spread_first_kernel,
        (band_shape, shape(F32, 1, width)),
        (col_index, row_length, part, ridge),
        smem=2,
    )
    if other is not None:
        band = call(
            spread_other_kernel, band_shape, (col_index, row_length, other, band), smem=2, aliases={3: 0}
        )
    distances = [1 << i for i in range(1, (devices - 1).bit_length())]
    pieces, message = (field,) * 3, shape(BF16, cols + 16, assets)

    to_near, to_far = call(products_first_kernel, (message,) * 2, (band, v0, ridge))
    qf0, qn0 = far(to_far), near(to_near)
    local0 = call(local_kernel, field, (band, together(v0, to_near)[0]))
    far0 = forward(together(near0, local0)[0])
    mean = together(mean, local0)[0]
    for distance in distances[1:-1]:
        mean = sum_step(mean, "asset", distance)
    mean, local0 = together(mean, local0)
    partial, means = call(
        gather_first_kernel, (field, shape(F32, 8, width)), (ridge, k0, local0, to_near, qn0, qf0)
    )
    k1, v1, before0, after0 = call(
        cross_first_kernel, (field, rounded, field, field), (band, partial, k0, means, near0, far0)
    )

    to_near1, to_far1 = call(products_second_kernel, (rounded, message), (band, v1, means))
    received, near1 = back(to_far1), near(v1)
    far1 = forward(near1)
    mean = sum_step(together(mean, to_near1)[0], "asset", distances[0])
    joined = call(add_kernel, message, (to_near1, received, mean))
    q1 = near(joined)
    local1 = call(local_kernel, field, (band, v1))
    partial, before1, after1 = call(
        cross_second_kernel,
        pieces,
        (band, ridge, means, k1, local0, local1, before0, after0, qn0, qf0, near1, far1),
    )
    k2, v2, mean = call(
        finish_second_kernel,
        (field, rounded, shape(F32, 1, width)),
        (k0, k1, means, partial, joined, q1),
    )

    to_near2, to_far2 = call(products_kernel, (rounded,) * 2, (band, v2))
    received2 = back(to_far2)
    local2 = call(local_kernel, field, (band, together(v2, to_near2)[0]), flops=5 * 10**9)
    near2 = near(together(v2, local2)[0])
    far2 = forward(near2)
    shift = sum_step(mean, "asset", distances[-1]) / devices
    out = shape(F32, assets, cols)
    known, rows1, rows2, share, both, field2 = call(
        settle_kernel,
        (field, out, out, shape(F32, 8, cols), field, field),
        (
            shift, means, ridge, k0, k1, k2, local0, local1, local2,
            before0, before1, after0, after1, qn0, qf0,
            m0, to_near2, to_near1, received, near1, near0,
        ),
    )
    joined, moments = call(
        form_kernel, (rounded, shape(F32, 8, cols)), (share, both, field2, received2, near2)
    )
    moments = sum_over(moments, "asset")
    q2 = near(joined)
    partial = call(cross_third_kernel, field, (band, known, near2, far2))
    rows3 = call(finish_third_kernel, out, (partial, q2))
    return call(
        combine_kernel,
        (out, out),
        (shift, moments, targets, rows1, rows2, rows3),
        scratch=[
            pltpu.VMEM((2, assets, cols), F32),
            pltpu.SemaphoreType.DMA((2, rows // 2)),
        ],
        results=HBM,
    )


def solution(mesh):
    return jax.shard_map(
        shards,
        mesh=mesh,
        in_specs=(
            P("asset", "rhs"),
            P("asset"),
            P("asset", None, "rhs", None),
            P("asset", None),
            P("asset"),
        ),
        out_specs=(P("asset", "rhs"), P("asset", "rhs")),
        check_vma=False,
    )
```

```python
import jax
import jax.numpy as jnp
from jax import lax
from jax.experimental import pallas as pl
from jax.experimental.pallas import tpu as pltpu
from jax.sharding import PartitionSpec as P

F32 = jnp.float32
BF16 = jnp.bfloat16
VMEM = pl.BlockSpec(memory_space=pltpu.VMEM)
SMEM = pl.BlockSpec(memory_space=pltpu.SMEM)
LIMIT = 8 * 1024 * 1024
HBM = pl.BlockSpec(memory_space=pltpu.HBM)
NN = (((1,), (0,)), ((), ()))
NT = (((1,), (1,)), ((), ()))


def call(kernel, out_shape, args, smem=0, outside=(), scratch=(), aliases=None, flops=0, results=VMEM):
    specs = [SMEM] * smem + [VMEM] * (len(args) - smem)
    for at in outside:
        specs[at] = HBM
    return pl.pallas_call(
        kernel,
        out_shape=out_shape,
        in_specs=specs,
        out_specs=jax.tree.map(lambda _: results, out_shape),
        scratch_shapes=scratch,
        input_output_aliases=aliases or {},
        cost_estimate=pl.CostEstimate(flops=flops, bytes_accessed=2**20, transcendentals=0) if flops else None,
        compiler_params=pltpu.CompilerParams(vmem_limit_bytes=LIMIT),
    )(*args)


def column_sums(values, width):
    folded = values[:, :width]
    for at in range(width, values.shape[1], width):
        folded = folded + values[:, at : at + width]
    return jnp.sum(folded.T, axis=0, keepdims=True)


def prepare_kernel(targets_ref, base_ref, rounded_ref, moment_ref):
    assets = targets_ref.shape[0]
    width = moment_ref.shape[1]
    for at in range(0, assets, width):
        tile = targets_ref[at : at + width, :].T
        base_ref[:, at : at + width] = tile
        rounded_ref[:, at : at + width] = tile.astype(BF16)
    values = targets_ref[...]
    moment_ref[...] = jnp.sum(values * values, axis=0, keepdims=True)


def place_blocks(col_ref, length_ref, offset, part_ref, band_ref):
    rows, slots, height, width = part_ref.shape
    spare = band_ref.shape[0] - 1
    total = rows * lax.axis_size("asset")
    first = lax.axis_index("asset") * rows - rows

    def one_row(row, carry):
        at = pl.ds(pl.multiple_of(row * width + offset, height), height)
        for slot in range(slots):
            place = col_ref[row, slot] - first
            place = jnp.where(place < 0, place + total, place)
            place = jnp.where(place >= total, place - total, place)
            place = jnp.where(slot < length_ref[row], place, spare)
            band_ref[place, at, :] = part_ref[row, slot]
        return carry

    lax.fori_loop(0, rows, one_row, 0)


def spread_first_kernel(col_ref, length_ref, part_ref, ridge_ref, band_ref, mean_ref):
    mean = jnp.sum(ridge_ref[...], axis=1, keepdims=True) / ridge_ref.shape[1]
    mean_ref[...] = jnp.broadcast_to(mean, mean_ref.shape)
    band_ref[...] = jnp.zeros_like(band_ref)
    height = part_ref.shape[2]
    mine = 0 if height == part_ref.shape[3] else lax.axis_index("rhs") * height
    place_blocks(col_ref, length_ref, mine, part_ref, band_ref)


def spread_other_kernel(col_ref, length_ref, part_ref, _, band_ref):
    height = part_ref.shape[2]
    place_blocks(col_ref, length_ref, (1 - lax.axis_index("rhs")) * height, part_ref, band_ref)


def is_odd(dims):
    return jnp.full(dims, lax.axis_index("asset") % 2, jnp.int32) == 1


def columns(ref, first, last, rows):
    return jnp.concatenate([ref[c, rows, :] for c in range(first, last)], axis=1)


def products_kernel(band_ref, v_ref, near_ref, far_ref):
    places, _, width = band_ref.shape
    rows = places // 3
    cols = v_ref.shape[0]
    odd = is_odd((cols, 2 * width))
    for j in range(0, rows, 2):
        out = slice(j * width, (j + 2) * width)
        low = slice(0, (j + 2) * width)
        high = slice(j * width, rows * width)
        before = lax.dot_general(
            v_ref[:, low], columns(band_ref, j, j + 2, low), NN, preferred_element_type=F32
        )
        after = lax.dot_general(
            v_ref[:, high],
            columns(band_ref, 2 * rows + j, 2 * rows + j + 2, high),
            NN,
            preferred_element_type=F32,
        )
        near_ref[:cols, out] = jnp.where(odd, before, after).astype(BF16)
        far_ref[:cols, out] = jnp.where(odd, after, before).astype(BF16)


def products_first_kernel(band_ref, v_ref, ridge_ref, near_ref, far_ref):
    products_kernel(band_ref, v_ref, near_ref, far_ref)
    cols, assets = v_ref.shape
    mean = jnp.sum(ridge_ref[...], axis=1, keepdims=True) / assets
    rest = jnp.broadcast_to(mean, (near_ref.shape[0] - cols, assets)).astype(BF16)
    near_ref[cols:, :] = rest
    far_ref[cols:, :] = rest


def products_second_kernel(band_ref, v_ref, mean_ref, near_ref, far_ref):
    products_kernel(band_ref, v_ref, near_ref, far_ref)
    cols = v_ref.shape[0]
    rest = (far_ref.shape[0] - cols, far_ref.shape[1])
    far_ref[cols:, :] = jnp.broadcast_to(mean_ref[0:1, 0:1], rest).astype(BF16)


def local_kernel(band_ref, v_ref, out_ref):
    places, _, width = band_ref.shape
    rows = places // 3
    cols = out_ref.shape[0]
    every = slice(0, rows * width)
    for j in range(0, rows, 2):
        out = slice(j * width, (j + 2) * width)
        out_ref[:, out] = lax.dot_general(
            v_ref[:cols, :],
            columns(band_ref, rows + j, rows + j + 2, every),
            NN,
            preferred_element_type=F32,
        ) + lax.dot_general(
            v_ref[:cols, :], columns(band_ref, rows, 2 * rows, out), NT, preferred_element_type=F32
        )


def neighbours(near_ref, far_ref, cols):
    near, far = near_ref[:cols, :].astype(F32), far_ref[:cols, :].astype(F32)
    odd = is_odd(near.shape)
    return jnp.where(odd, near, far).astype(BF16), jnp.where(odd, far, near).astype(BF16)


def forward_products(band_ref, before, after, j):
    places, _, width = band_ref.shape
    rows = places // 3
    out = slice(j * width, (j + 2) * width)
    return out, lax.dot_general(
        before[:, j * width :], columns(band_ref, j, rows, out), NT, preferred_element_type=F32
    ), lax.dot_general(
        after[:, : (j + 2) * width],
        columns(band_ref, 2 * rows, 2 * rows + j + 2, out),
        NT,
        preferred_element_type=F32,
    )


def gather_first_kernel(ridge_ref, k_ref, local_ref, own_ref, near_ref, far_ref, sum_ref, mean_ref):
    cols, width = k_ref.shape[0], mean_ref.shape[1]
    means = [ref[cols : cols + 16, :width].astype(F32)[:1] for ref in (own_ref, near_ref, far_ref)]
    odd = is_odd(means[0].shape)
    means += [jnp.where(odd, means[1], means[2]), jnp.where(odd, means[2], means[1])]
    means.append(means[0] + means[1])
    for i, value in enumerate(means):
        mean_ref[i : i + 1, :] = value
    both = local_ref[...] + near_ref[:cols, :].astype(F32) + far_ref[:cols, :].astype(F32)
    sum_ref[...] = ridge_ref[...] * k_ref[...] + 0.5 * both


def cross_first_kernel(
    band_ref, sum_ref, k_ref, mean_ref, near_ref, far_ref, next_ref, rounded_ref, before_ref, after_ref
):
    before, after = neighbours(near_ref, far_ref, k_ref.shape[0])
    for j in range(0, band_ref.shape[0] // 3, 2):
        out, first, second = forward_products(band_ref, before, after, j)
        before_ref[:, out] = first
        after_ref[:, out] = second
        value = sum_ref[:, out] + 0.5 * (first + second)
        next_ref[:, out] = value
        rounded_ref[:, out] = (value - mean_ref[0:1, 0:1] * k_ref[:, out]).astype(BF16)


def cross_second_kernel(
    band_ref, ridge_ref, mean_ref, k_ref, local0_ref, local_ref, before0_ref, after0_ref, qn0_ref, qf0_ref,
    near_ref, far_ref, sum_ref, before_ref, after_ref
):
    own, mean_near, mean_far, mean_before, mean_after = (mean_ref[i : i + 1, 0:1] for i in range(5))
    before, after = neighbours(near_ref, far_ref, k_ref.shape[0])
    for j in range(0, band_ref.shape[0] // 3, 2):
        out, first, second = forward_products(band_ref, before, after, j)
        before_ref[:, out] = first
        after_ref[:, out] = second
        known = own * local0_ref[:, out] + mean_before * before0_ref[:, out] + mean_after * after0_ref[:, out]
        known = known + mean_near * qn0_ref[: k_ref.shape[0], out].astype(F32) + mean_far * qf0_ref[: k_ref.shape[0], out].astype(F32)
        both = local_ref[:, out] + first + second + known
        sum_ref[:, out] = ridge_ref[:, out] * k_ref[:, out] + 0.5 * both


def finish_second_kernel(
    k0_ref, k_ref, mean_ref, sum_ref, own_ref, q_ref, next_ref, rounded_ref, total_ref
):
    cols, width = k_ref.shape[0], total_ref.shape[1]
    sums = [ref[cols : cols + 16, :width].astype(F32)[:1] for ref in (own_ref, q_ref)]
    total_ref[...] = sums[0] + sums[1]
    value = sum_ref[...] + 0.5 * q_ref[:cols, :].astype(F32)
    next_ref[...] = value
    own = mean_ref[0:1, 0:1]
    rounded_ref[...] = (value - 2 * own * k_ref[...] + own * own * k0_ref[...]).astype(BF16)


def settle_kernel(
    shift_ref, mean_ref, ridge_ref, k0_ref, k1_ref, k2_ref, local0_ref, local1_ref, local2_ref,
    before0_ref, before1_ref, after0_ref, after1_ref, qn0_ref, qf0_ref,
    m0_ref, to2_ref, to1_ref, r1_ref, near1_ref, near0_ref,
    sum_ref, rows1_ref, rows2_ref, moment_ref, both_ref, field_ref
):
    cols, width = k0_ref.shape[0], moment_ref.shape[1]
    c = shift_ref[0:1, 0:1]
    own, mean_near, mean_far, mean_before, mean_after = (mean_ref[i : i + 1, 0:1] - c for i in range(5))
    other = r1_ref[cols : cols + 16, :width].astype(F32)[:1, :1] - c
    totals = [jnp.zeros((cols, width), F32)] * 5
    for at in range(0, k0_ref.shape[1], width):
        out = slice(at, at + width)
        k0, k1 = k0_ref[:, out], k1_ref[:, out]
        s1 = k1 - c * k0
        s2 = k2_ref[:, out] - 2 * c * k1 + c * c * k0
        rows1_ref[out, :] = s1.T
        rows2_ref[out, :] = s2.T
        local = local2_ref[:, out] + 2 * own * local1_ref[:, out] + own * own * local0_ref[:, out]
        mine = (ridge_ref[:, out] - c) * s2 + 0.5 * local
        known = 2 * mean_before * before1_ref[:, out] + mean_before * mean_before * before0_ref[:, out]
        known = known + 2 * mean_after * after1_ref[:, out] + mean_after * mean_after * after0_ref[:, out]
        back = mean_near * mean_near * qn0_ref[:cols, out].astype(F32)
        back = back + mean_far * mean_far * qf0_ref[:cols, out].astype(F32)
        sum_ref[:, out] = mine + 0.5 * (known + back)
        both = to2_ref[:, out].astype(F32) + 2 * own * to1_ref[:, out].astype(F32)
        both_ref[:, out] = both + 2 * other * r1_ref[:cols, out].astype(F32)
        field = 2 * mean_near * near1_ref[:, out].astype(F32)
        field_ref[:, out] = field + mean_near * mean_near * near0_ref[:, out].astype(F32)
        parts = (k0 * s1, s1 * s1, s1 * s2, s2 * s2, s2 * (mine + back))
        totals = [total + part for total, part in zip(totals, parts, strict=True)]
    moment_ref[0:1, :] = m0_ref[...]
    for i, total in enumerate(totals):
        moment_ref[i + 1 : i + 2, :] = jnp.sum(total.T, axis=0, keepdims=True)
    moment_ref[6:8, :] = jnp.zeros((2, width), F32)


def form_kernel(share_ref, both_ref, field_ref, received_ref, near_ref, q_ref, moment_ref):
    cols, assets = both_ref.shape
    width = moment_ref.shape[1]
    total = jnp.zeros((cols, width), F32)
    for at in range(0, assets, width):
        out = slice(at, at + width)
        both = both_ref[:, out] + received_ref[:, out].astype(F32)
        q_ref[:, out] = both.astype(BF16)
        total = total + both * (field_ref[:, out] + near_ref[:, out].astype(F32))
    moment_ref[...] = share_ref[...]
    moment_ref[5:6, :] = share_ref[5:6, :] + jnp.sum(total.T, axis=0, keepdims=True)


def cross_third_kernel(band_ref, known_ref, near_ref, far_ref, sum_ref):
    before, after = neighbours(near_ref, far_ref, known_ref.shape[0])
    for j in range(0, band_ref.shape[0] // 3, 2):
        out, first, second = forward_products(band_ref, before, after, j)
        sum_ref[:, out] = known_ref[:, out] + 0.5 * (first + second)


def finish_third_kernel(sum_ref, q_ref, rows3_ref):
    width = rows3_ref.shape[1]
    for at in range(0, sum_ref.shape[1], width):
        out = slice(at, at + width)
        rows3_ref[out, :] = (sum_ref[:, out] + 0.5 * q_ref[:, out].astype(F32)).T


def ratio(above, below):
    return jnp.where(below == 0, 0.0, above / below)


def scalars(m, shift, iters):
    zero = jnp.zeros_like(m[0])
    solution = [zero] * iters
    residual = [zero + 1.0] + [zero] * iters
    direction = [zero + 1.0] + [zero] * (iters - 1)

    def inner(a, b):
        total = zero
        for i, left in enumerate(a):
            for j, right in enumerate(b):
                if i + j < len(m):
                    total = total + left * right * m[i + j]
        return total

    now = m[0]
    for step in range(iters):
        used = direction[: step + 1]
        image = [shift * value for value in used] + [zero]
        for i, value in enumerate(used):
            image[i + 1] = image[i + 1] + value
        alpha = ratio(now, inner(used, image))
        for i, value in enumerate(used):
            solution[i] = solution[i] + alpha * value
        for i, value in enumerate(image):
            residual[i] = residual[i] - alpha * value
        if step + 1 < iters:
            left = residual[: step + 2]
            new = inner(left, left)
            beta = ratio(new, now)
            direction = [r + beta * d for r, d in zip(residual[:iters], direction, strict=True)]
            now = new
    return solution, residual


def combine_kernel(
    shift_ref, moment_ref, targets_ref, k1_ref, k2_ref, k3_ref, solution_hbm, residual_hbm, held, sems
):
    width = moment_ref.shape[1]
    m = [moment_ref[i : i + 1, :] for i in range(6)]
    x, r = scalars(m, shift_ref[...], 3)
    assets = targets_ref.shape[0]
    size = 2 * width
    copies = []
    for part in range(assets // size):
        out = slice(part * size, (part + 1) * size)
        k0, k1, k2, k3 = targets_ref[out, :], k1_ref[out, :], k2_ref[out, :], k3_ref[out, :]
        held[0, out, :] = x[0] * k0 + x[1] * k1 + x[2] * k2
        held[1, out, :] = r[0] * k0 + r[1] * k1 + r[2] * k2 + r[3] * k3
        for i, target in enumerate((solution_hbm, residual_hbm)):
            copy = pltpu.make_async_copy(held.at[i, out, :], target.at[out, :], sems.at[i, part])
            copy.start()
            copies.append(copy)
    for copy in copies:
        copy.wait()


def near(value):
    count = lax.axis_size("asset")
    return lax.ppermute(value, "asset", [(i, i ^ 1) for i in range(count)])


def far(value):
    count = lax.axis_size("asset")
    return lax.ppermute(
        value, "asset", [(i, (i + 1 if i % 2 else i - 1) % count) for i in range(count)]
    )


def forward(value):
    count = lax.axis_size("asset")
    return lax.ppermute(
        value, "asset", [(i, (i - 2 if i % 2 else i + 2) % count) for i in range(count)]
    )


def back(value):
    count = lax.axis_size("asset")
    return lax.ppermute(
        value, "asset", [(i, (i + 2 if i % 2 else i - 2) % count) for i in range(count)]
    )


def add_kernel(near_ref, received_ref, mean_ref, out_ref):
    cols = near_ref.shape[0]
    out_ref[:cols, :] = (near_ref[...].astype(F32) + received_ref[:cols, :].astype(F32)).astype(BF16)
    rest = (out_ref.shape[0] - cols, out_ref.shape[1])
    out_ref[cols:, :] = jnp.broadcast_to(mean_ref[0:1, 0:1], rest).astype(BF16)


def sum_step(value, axis, distance):
    count = lax.axis_size(axis)
    return value + lax.ppermute(value, axis, [(i, i ^ distance) for i in range(count)])


def sum_over(value, axis):
    count = lax.axis_size(axis)
    step = 1
    while step < count:
        total = value
        for distance in (step, 2 * step, 3 * step) if 2 * step < count else (step,):
            route = [(i, i ^ distance) for i in range(count)]
            total = total + lax.ppermute(value, axis, route)
        value = total
        step *= 4
    return value


def together(*values):
    return lax.optimization_barrier(values)


def shards(targets, ridge, blocks, col_index, row_length):
    rows, slots, height, width = blocks.shape
    cols = targets.shape[1]
    assets = rows * width
    devices = lax.axis_size("asset")
    halves = lax.axis_size("rhs")
    ridge = ridge[None, :]

    def shape(kind, *dims):
        return jax.ShapeDtypeStruct(dims, kind)

    field, rounded, row = shape(F32, cols, assets), shape(BF16, cols, assets), shape(F32, 1, cols)
    band_shape = shape(BF16, 3 * rows + 1, assets, width)
    if halves == 2:
        part, other = blocks, lax.ppermute(blocks, "rhs", [(0, 1), (1, 0)])
    else:
        part, other = lax.all_gather(blocks, "rhs", axis=2, tiled=True), None

    k0, v0, m0 = call(prepare_kernel, (field, rounded, row), (targets,), flops=5 * 10**9)
    near0 = near(v0)
    band, mean = call(
        spread_first_kernel,
        (band_shape, shape(F32, 1, width)),
        (col_index, row_length, part, ridge),
        smem=2,
    )
    if other is not None:
        band = call(
            spread_other_kernel, band_shape, (col_index, row_length, other, band), smem=2, aliases={3: 0}
        )
    distances = [1 << i for i in range(1, (devices - 1).bit_length())]
    pieces, message = (field,) * 3, shape(BF16, cols + 16, assets)

    to_near, to_far = call(products_first_kernel, (message,) * 2, (band, v0, ridge))
    qf0, qn0 = far(to_far), near(to_near)
    local0 = call(local_kernel, field, (band, together(v0, to_near)[0]))
    far0 = forward(together(near0, local0)[0])
    mean = together(mean, local0)[0]
    for distance in distances[1:-1]:
        mean = sum_step(mean, "asset", distance)
    mean, local0 = together(mean, local0)
    partial, means = call(
        gather_first_kernel, (field, shape(F32, 8, width)), (ridge, k0, local0, to_near, qn0, qf0)
    )
    k1, v1, before0, after0 = call(
        cross_first_kernel, (field, rounded, field, field), (band, partial, k0, means, near0, far0)
    )

    to_near1, to_far1 = call(products_second_kernel, (rounded, message), (band, v1, means))
    received, near1 = back(to_far1), near(v1)
    far1 = forward(near1)
    mean = sum_step(together(mean, to_near1)[0], "asset", distances[0])
    joined = call(add_kernel, message, (to_near1, received, mean))
    q1 = near(joined)
    local1 = call(local_kernel, field, (band, v1))
    partial, before1, after1 = call(
        cross_second_kernel,
        pieces,
        (band, ridge, means, k1, local0, local1, before0, after0, qn0, qf0, near1, far1),
    )
    k2, v2, mean = call(
        finish_second_kernel,
        (field, rounded, shape(F32, 1, width)),
        (k0, k1, means, partial, joined, q1),
    )

    to_near2, to_far2 = call(products_kernel, (rounded,) * 2, (band, v2))
    received2 = back(to_far2)
    local2 = call(local_kernel, field, (band, together(v2, to_near2)[0]), flops=5 * 10**9)
    near2 = near(together(v2, local2)[0])
    far2 = forward(near2)
    shift = sum_step(mean, "asset", distances[-1]) / devices
    out = shape(F32, assets, cols)
    known, rows1, rows2, share, both, field2 = call(
        settle_kernel,
        (field, out, out, shape(F32, 8, cols), field, field),
        (
            shift, means, ridge, k0, k1, k2, local0, local1, local2,
            before0, before1, after0, after1, qn0, qf0,
            m0, to_near2, to_near1, received, near1, near0,
        ),
    )
    joined, moments = call(
        form_kernel, (rounded, shape(F32, 8, cols)), (share, both, field2, received2, near2)
    )
    moments = sum_over(moments, "asset")
    q2 = near(joined)
    partial = call(cross_third_kernel, field, (band, known, near2, far2))
    rows3 = call(finish_third_kernel, out, (partial, q2))
    return call(
        combine_kernel,
        (out, out),
        (shift, moments, targets, rows1, rows2, rows3),
        scratch=[
            pltpu.VMEM((2, assets, cols), F32),
            pltpu.SemaphoreType.DMA((2, rows // 2)),
        ],
        results=HBM,
    )


def solution(mesh):
    return jax.shard_map(
        shards,
        mesh=mesh,
        in_specs=(
            P("asset", "rhs"),
            P("asset"),
            P("asset", None, "rhs", None),
            P("asset", None),
            P("asset"),
        ),
        out_specs=(P("asset", "rhs"), P("asset", "rhs")),
        check_vma=False,
    )
```

```python
import jax
import jax.numpy as jnp
from jax import lax
from jax.experimental import pallas as pl
from jax.experimental.pallas import tpu as pltpu
from jax.sharding import PartitionSpec as P

F32 = jnp.float32
BF16 = jnp.bfloat16
VMEM = pl.BlockSpec(memory_space=pltpu.VMEM)
SMEM = pl.BlockSpec(memory_space=pltpu.SMEM)
LIMIT = 8 * 1024 * 1024
HBM = pl.BlockSpec(memory_space=pltpu.HBM)
NN = (((1,), (0,)), ((), ()))
NT = (((1,), (1,)), ((), ()))


def call(kernel, out_shape, args, smem=0, outside=(), scratch=(), aliases=None, flops=0, results=VMEM):
    specs = [SMEM] * smem + [VMEM] * (len(args) - smem)
    for at in outside:
        specs[at] = HBM
    return pl.pallas_call(
        kernel,
        out_shape=out_shape,
        in_specs=specs,
        out_specs=jax.tree.map(lambda _: results, out_shape),
        scratch_shapes=scratch,
        input_output_aliases=aliases or {},
        cost_estimate=pl.CostEstimate(flops=flops, bytes_accessed=2**20, transcendentals=0) if flops else None,
        compiler_params=pltpu.CompilerParams(vmem_limit_bytes=LIMIT),
    )(*args)


def column_sums(values, width):
    folded = values[:, :width]
    for at in range(width, values.shape[1], width):
        folded = folded + values[:, at : at + width]
    return jnp.sum(folded.T, axis=0, keepdims=True)


def prepare_kernel(targets_ref, base_ref, rounded_ref, moment_ref):
    assets = targets_ref.shape[0]
    width = moment_ref.shape[1]
    for at in range(0, assets, width):
        tile = targets_ref[at : at + width, :].T
        base_ref[:, at : at + width] = tile
        rounded_ref[:, at : at + width] = tile.astype(BF16)
    values = targets_ref[...]
    moment_ref[...] = jnp.sum(values * values, axis=0, keepdims=True)


def place_blocks(col_ref, length_ref, offset, part_ref, band_ref):
    rows, slots, height, width = part_ref.shape
    spare = band_ref.shape[0] - 1
    total = rows * lax.axis_size("asset")
    first = lax.axis_index("asset") * rows - rows

    def one_row(row, carry):
        at = pl.ds(pl.multiple_of(row * width + offset, height), height)
        for slot in range(slots):
            place = col_ref[row, slot] - first
            place = jnp.where(place < 0, place + total, place)
            place = jnp.where(place >= total, place - total, place)
            place = jnp.where(slot < length_ref[row], place, spare)
            band_ref[place, at, :] = part_ref[row, slot]
        return carry

    lax.fori_loop(0, rows, one_row, 0)


def spread_first_kernel(col_ref, length_ref, part_ref, ridge_ref, band_ref, mean_ref):
    mean = jnp.sum(ridge_ref[...], axis=1, keepdims=True) / ridge_ref.shape[1]
    mean_ref[...] = jnp.broadcast_to(mean, mean_ref.shape)
    band_ref[...] = jnp.zeros_like(band_ref)
    height = part_ref.shape[2]
    mine = 0 if height == part_ref.shape[3] else lax.axis_index("rhs") * height
    place_blocks(col_ref, length_ref, mine, part_ref, band_ref)


def spread_other_kernel(col_ref, length_ref, part_ref, _, band_ref):
    height = part_ref.shape[2]
    place_blocks(col_ref, length_ref, (1 - lax.axis_index("rhs")) * height, part_ref, band_ref)


def is_odd(dims):
    return jnp.full(dims, lax.axis_index("asset") % 2, jnp.int32) == 1


def columns(ref, first, last, rows):
    return jnp.concatenate([ref[c, rows, :] for c in range(first, last)], axis=1)


def products_kernel(band_ref, v_ref, near_ref, far_ref):
    places, _, width = band_ref.shape
    rows = places // 3
    cols = v_ref.shape[0]
    odd = is_odd((cols, 2 * width))
    for j in range(0, rows, 2):
        out = slice(j * width, (j + 2) * width)
        low = slice(0, (j + 2) * width)
        high = slice(j * width, rows * width)
        before = lax.dot_general(
            v_ref[:, low], columns(band_ref, j, j + 2, low), NN, preferred_element_type=F32
        )
        after = lax.dot_general(
            v_ref[:, high],
            columns(band_ref, 2 * rows + j, 2 * rows + j + 2, high),
            NN,
            preferred_element_type=F32,
        )
        near_ref[:cols, out] = jnp.where(odd, before, after).astype(BF16)
        far_ref[:cols, out] = jnp.where(odd, after, before).astype(BF16)


def products_first_kernel(band_ref, v_ref, ridge_ref, near_ref, far_ref):
    products_kernel(band_ref, v_ref, near_ref, far_ref)
    cols, assets = v_ref.shape
    mean = jnp.sum(ridge_ref[...], axis=1, keepdims=True) / assets
    rest = jnp.broadcast_to(mean, (near_ref.shape[0] - cols, assets)).astype(BF16)
    near_ref[cols:, :] = rest
    far_ref[cols:, :] = rest


def products_second_kernel(band_ref, v_ref, mean_ref, near_ref, far_ref):
    products_kernel(band_ref, v_ref, near_ref, far_ref)
    cols = v_ref.shape[0]
    rest = (far_ref.shape[0] - cols, far_ref.shape[1])
    far_ref[cols:, :] = jnp.broadcast_to(mean_ref[0:1, 0:1], rest).astype(BF16)


def local_kernel(band_ref, v_ref, out_ref):
    places, _, width = band_ref.shape
    rows = places // 3
    cols = out_ref.shape[0]
    every = slice(0, rows * width)
    for j in range(0, rows, 2):
        out = slice(j * width, (j + 2) * width)
        out_ref[:, out] = lax.dot_general(
            v_ref[:cols, :],
            columns(band_ref, rows + j, rows + j + 2, every),
            NN,
            preferred_element_type=F32,
        ) + lax.dot_general(
            v_ref[:cols, :], columns(band_ref, rows, 2 * rows, out), NT, preferred_element_type=F32
        )


def neighbours(near_ref, far_ref, cols):
    near, far = near_ref[:cols, :].astype(F32), far_ref[:cols, :].astype(F32)
    odd = is_odd(near.shape)
    return jnp.where(odd, near, far).astype(BF16), jnp.where(odd, far, near).astype(BF16)


def forward_products(band_ref, before, after, j):
    places, _, width = band_ref.shape
    rows = places // 3
    out = slice(j * width, (j + 2) * width)
    return out, lax.dot_general(
        before[:, j * width :], columns(band_ref, j, rows, out), NT, preferred_element_type=F32
    ), lax.dot_general(
        after[:, : (j + 2) * width],
        columns(band_ref, 2 * rows, 2 * rows + j + 2, out),
        NT,
        preferred_element_type=F32,
    )


def gather_first_kernel(ridge_ref, k_ref, local_ref, own_ref, near_ref, far_ref, sum_ref, mean_ref):
    cols, width = k_ref.shape[0], mean_ref.shape[1]
    means = [ref[cols : cols + 16, :width].astype(F32)[:1] for ref in (own_ref, near_ref, far_ref)]
    odd = is_odd(means[0].shape)
    means += [jnp.where(odd, means[1], means[2]), jnp.where(odd, means[2], means[1])]
    means.append(means[0] + means[1])
    for i, value in enumerate(means):
        mean_ref[i : i + 1, :] = value
    both = local_ref[...] + near_ref[:cols, :].astype(F32) + far_ref[:cols, :].astype(F32)
    sum_ref[...] = ridge_ref[...] * k_ref[...] + 0.5 * both


def cross_first_kernel(
    band_ref, sum_ref, k_ref, mean_ref, near_ref, far_ref, next_ref, rounded_ref, before_ref, after_ref
):
    before, after = neighbours(near_ref, far_ref, k_ref.shape[0])
    for j in range(0, band_ref.shape[0] // 3, 2):
        out, first, second = forward_products(band_ref, before, after, j)
        before_ref[:, out] = first
        after_ref[:, out] = second
        value = sum_ref[:, out] + 0.5 * (first + second)
        next_ref[:, out] = value
        rounded_ref[:, out] = (value - mean_ref[0:1, 0:1] * k_ref[:, out]).astype(BF16)


def cross_second_kernel(
    band_ref, ridge_ref, mean_ref, k_ref, local0_ref, local_ref, before0_ref, after0_ref, qn0_ref, qf0_ref,
    near_ref, far_ref, sum_ref, before_ref, after_ref
):
    own, mean_near, mean_far, mean_before, mean_after = (mean_ref[i : i + 1, 0:1] for i in range(5))
    before, after = neighbours(near_ref, far_ref, k_ref.shape[0])
    for j in range(0, band_ref.shape[0] // 3, 2):
        out, first, second = forward_products(band_ref, before, after, j)
        before_ref[:, out] = first
        after_ref[:, out] = second
        known = own * local0_ref[:, out] + mean_before * before0_ref[:, out] + mean_after * after0_ref[:, out]
        known = known + mean_near * qn0_ref[: k_ref.shape[0], out].astype(F32) + mean_far * qf0_ref[: k_ref.shape[0], out].astype(F32)
        both = local_ref[:, out] + first + second + known
        sum_ref[:, out] = ridge_ref[:, out] * k_ref[:, out] + 0.5 * both


def finish_second_kernel(
    k0_ref, k_ref, mean_ref, sum_ref, own_ref, q_ref, next_ref, rounded_ref, total_ref
):
    cols, width = k_ref.shape[0], total_ref.shape[1]
    sums = [ref[cols : cols + 16, :width].astype(F32)[:1] for ref in (own_ref, q_ref)]
    total_ref[...] = sums[0] + sums[1]
    value = sum_ref[...] + 0.5 * q_ref[:cols, :].astype(F32)
    next_ref[...] = value
    own = mean_ref[0:1, 0:1]
    rounded_ref[...] = (value - 2 * own * k_ref[...] + own * own * k0_ref[...]).astype(BF16)


def settle_kernel(
    shift_ref, mean_ref, ridge_ref, k0_ref, k1_ref, k2_ref, local0_ref, local1_ref, local2_ref,
    before0_ref, before1_ref, after0_ref, after1_ref, qn0_ref, qf0_ref,
    m0_ref, to2_ref, to1_ref, r1_ref, near1_ref, near0_ref,
    sum_ref, rows1_ref, rows2_ref, moment_ref, both_ref, field_ref
):
    cols, width = k0_ref.shape[0], moment_ref.shape[1]
    c = shift_ref[0:1, 0:1]
    own, mean_near, mean_far, mean_before, mean_after = (mean_ref[i : i + 1, 0:1] - c for i in range(5))
    other = r1_ref[cols : cols + 16, :width].astype(F32)[:1, :1] - c
    totals = [jnp.zeros((cols, width), F32)] * 5
    for at in range(0, k0_ref.shape[1], width):
        out = slice(at, at + width)
        k0, k1 = k0_ref[:, out], k1_ref[:, out]
        s1 = k1 - c * k0
        s2 = k2_ref[:, out] - 2 * c * k1 + c * c * k0
        rows1_ref[out, :] = s1.T
        rows2_ref[out, :] = s2.T
        local = local2_ref[:, out] + 2 * own * local1_ref[:, out] + own * own * local0_ref[:, out]
        mine = (ridge_ref[:, out] - c) * s2 + 0.5 * local
        known = 2 * mean_before * before1_ref[:, out] + mean_before * mean_before * before0_ref[:, out]
        known = known + 2 * mean_after * after1_ref[:, out] + mean_after * mean_after * after0_ref[:, out]
        back = mean_near * mean_near * qn0_ref[:cols, out].astype(F32)
        back = back + mean_far * mean_far * qf0_ref[:cols, out].astype(F32)
        sum_ref[:, out] = mine + 0.5 * (known + back)
        both = to2_ref[:, out].astype(F32) + 2 * own * to1_ref[:, out].astype(F32)
        both_ref[:, out] = both + 2 * other * r1_ref[:cols, out].astype(F32)
        field = 2 * mean_near * near1_ref[:, out].astype(F32)
        field_ref[:, out] = field + mean_near * mean_near * near0_ref[:, out].astype(F32)
        parts = (k0 * s1, s1 * s1, s1 * s2, s2 * s2, s2 * (mine + back))
        totals = [total + part for total, part in zip(totals, parts, strict=True)]
    moment_ref[0:1, :] = m0_ref[...]
    for i, total in enumerate(totals):
        moment_ref[i + 1 : i + 2, :] = jnp.sum(total.T, axis=0, keepdims=True)
    moment_ref[6:8, :] = jnp.zeros((2, width), F32)


def form_kernel(share_ref, both_ref, field_ref, received_ref, near_ref, q_ref, moment_ref):
    cols, assets = both_ref.shape
    width = moment_ref.shape[1]
    total = jnp.zeros((cols, width), F32)
    for at in range(0, assets, width):
        out = slice(at, at + width)
        both = both_ref[:, out] + received_ref[:, out].astype(F32)
        q_ref[:, out] = both.astype(BF16)
        total = total + both * (field_ref[:, out] + near_ref[:, out].astype(F32))
    moment_ref[...] = share_ref[...]
    moment_ref[5:6, :] = share_ref[5:6, :] + jnp.sum(total.T, axis=0, keepdims=True)


def cross_third_kernel(band_ref, known_ref, near_ref, far_ref, sum_ref):
    before, after = neighbours(near_ref, far_ref, known_ref.shape[0])
    for j in range(0, band_ref.shape[0] // 3, 2):
        out, first, second = forward_products(band_ref, before, after, j)
        sum_ref[:, out] = known_ref[:, out] + 0.5 * (first + second)


def ratio(above, below):
    return jnp.where(below == 0, 0.0, above / below)


def scalars(m, shift, iters):
    zero = jnp.zeros_like(m[0])
    solution = [zero] * iters
    residual = [zero + 1.0] + [zero] * iters
    direction = [zero + 1.0] + [zero] * (iters - 1)

    def inner(a, b):
        total = zero
        for i, left in enumerate(a):
            for j, right in enumerate(b):
                if i + j < len(m):
                    total = total + left * right * m[i + j]
        return total

    now = m[0]
    for step in range(iters):
        used = direction[: step + 1]
        image = [shift * value for value in used] + [zero]
        for i, value in enumerate(used):
            image[i + 1] = image[i + 1] + value
        alpha = ratio(now, inner(used, image))
        for i, value in enumerate(used):
            solution[i] = solution[i] + alpha * value
        for i, value in enumerate(image):
            residual[i] = residual[i] - alpha * value
        if step + 1 < iters:
            left = residual[: step + 2]
            new = inner(left, left)
            beta = ratio(new, now)
            direction = [r + beta * d for r, d in zip(residual[:iters], direction, strict=True)]
            now = new
    return solution, residual


def combine_kernel(
    shift_ref, moment_ref, targets_ref, k1_ref, k2_ref, sum_ref, q_ref, solution_hbm, residual_hbm, held, sems
):
    width = moment_ref.shape[1]
    m = [moment_ref[i : i + 1, :] for i in range(6)]
    x, r = scalars(m, shift_ref[...], 3)
    assets = targets_ref.shape[0]
    size = 2 * width
    copies = []
    for part in range(assets // size):
        out = slice(part * size, (part + 1) * size)
        k0, k1, k2 = targets_ref[out, :], k1_ref[out, :], k2_ref[out, :]
        k3 = (sum_ref[:, out] + 0.5 * q_ref[:, out].astype(F32)).T
        held[0, out, :] = x[0] * k0 + x[1] * k1 + x[2] * k2
        held[1, out, :] = r[0] * k0 + r[1] * k1 + r[2] * k2 + r[3] * k3
        for i, target in enumerate((solution_hbm, residual_hbm)):
            copy = pltpu.make_async_copy(held.at[i, out, :], target.at[out, :], sems.at[i, part])
            copy.start()
            copies.append(copy)
    for copy in copies:
        copy.wait()


def near(value):
    count = lax.axis_size("asset")
    return lax.ppermute(value, "asset", [(i, i ^ 1) for i in range(count)])


def far(value):
    count = lax.axis_size("asset")
    return lax.ppermute(
        value, "asset", [(i, (i + 1 if i % 2 else i - 1) % count) for i in range(count)]
    )


def forward(value):
    count = lax.axis_size("asset")
    return lax.ppermute(
        value, "asset", [(i, (i - 2 if i % 2 else i + 2) % count) for i in range(count)]
    )


def back(value):
    count = lax.axis_size("asset")
    return lax.ppermute(
        value, "asset", [(i, (i + 2 if i % 2 else i - 2) % count) for i in range(count)]
    )


def add_kernel(near_ref, received_ref, mean_ref, out_ref):
    cols = near_ref.shape[0]
    out_ref[:cols, :] = (near_ref[...].astype(F32) + received_ref[:cols, :].astype(F32)).astype(BF16)
    rest = (out_ref.shape[0] - cols, out_ref.shape[1])
    out_ref[cols:, :] = jnp.broadcast_to(mean_ref[0:1, 0:1], rest).astype(BF16)


def sum_step(value, axis, distance):
    count = lax.axis_size(axis)
    return value + lax.ppermute(value, axis, [(i, i ^ distance) for i in range(count)])


def sum_over(value, axis):
    count = lax.axis_size(axis)
    step = 1
    while step < count:
        total = value
        for distance in (step, 2 * step, 3 * step) if 2 * step < count else (step,):
            route = [(i, i ^ distance) for i in range(count)]
            total = total + lax.ppermute(value, axis, route)
        value = total
        step *= 4
    return value


def together(*values):
    return lax.optimization_barrier(values)


def shards(targets, ridge, blocks, col_index, row_length):
    rows, slots, height, width = blocks.shape
    cols = targets.shape[1]
    assets = rows * width
    devices = lax.axis_size("asset")
    halves = lax.axis_size("rhs")
    ridge = ridge[None, :]

    def shape(kind, *dims):
        return jax.ShapeDtypeStruct(dims, kind)

    field, rounded, row = shape(F32, cols, assets), shape(BF16, cols, assets), shape(F32, 1, cols)
    band_shape = shape(BF16, 3 * rows + 1, assets, width)
    if halves == 2:
        part, other = blocks, lax.ppermute(blocks, "rhs", [(0, 1), (1, 0)])
    else:
        part, other = lax.all_gather(blocks, "rhs", axis=2, tiled=True), None

    k0, v0, m0 = call(prepare_kernel, (field, rounded, row), (targets,), flops=5 * 10**9)
    near0 = near(v0)
    band, mean = call(
        spread_first_kernel,
        (band_shape, shape(F32, 1, width)),
        (col_index, row_length, part, ridge),
        smem=2,
    )
    if other is not None:
        band = call(
            spread_other_kernel, band_shape, (col_index, row_length, other, band), smem=2, aliases={3: 0}
        )
    distances = [1 << i for i in range(1, (devices - 1).bit_length())]
    pieces, message = (field,) * 3, shape(BF16, cols + 16, assets)

    to_near, to_far = call(products_first_kernel, (message,) * 2, (band, v0, ridge))
    qf0, qn0 = far(to_far), near(to_near)
    local0 = call(local_kernel, field, (band, together(v0, to_near)[0]))
    far0 = forward(together(near0, local0)[0])
    mean = together(mean, local0)[0]
    for distance in distances[1:-1]:
        mean = sum_step(mean, "asset", distance)
    mean, local0 = together(mean, local0)
    partial, means = call(
        gather_first_kernel, (field, shape(F32, 8, width)), (ridge, k0, local0, to_near, qn0, qf0)
    )
    k1, v1, before0, after0 = call(
        cross_first_kernel, (field, rounded, field, field), (band, partial, k0, means, near0, far0)
    )

    to_near1, to_far1 = call(products_second_kernel, (rounded, message), (band, v1, means))
    received, near1 = back(to_far1), near(v1)
    far1 = forward(near1)
    mean = sum_step(together(mean, to_near1)[0], "asset", distances[0])
    joined = call(add_kernel, message, (to_near1, received, mean))
    q1 = near(joined)
    local1 = call(local_kernel, field, (band, v1))
    partial, before1, after1 = call(
        cross_second_kernel,
        pieces,
        (band, ridge, means, k1, local0, local1, before0, after0, qn0, qf0, near1, far1),
    )
    k2, v2, mean = call(
        finish_second_kernel,
        (field, rounded, shape(F32, 1, width)),
        (k0, k1, means, partial, joined, q1),
    )

    to_near2, to_far2 = call(products_kernel, (rounded,) * 2, (band, v2))
    received2 = back(to_far2)
    local2 = call(local_kernel, field, (band, together(v2, to_near2)[0]), flops=5 * 10**9)
    near2 = near(together(v2, local2)[0])
    far2 = forward(near2)
    shift = sum_step(mean, "asset", distances[-1]) / devices
    out = shape(F32, assets, cols)
    known, rows1, rows2, share, both, field2 = call(
        settle_kernel,
        (field, out, out, shape(F32, 8, cols), field, field),
        (
            shift, means, ridge, k0, k1, k2, local0, local1, local2,
            before0, before1, after0, after1, qn0, qf0,
            m0, to_near2, to_near1, received, near1, near0,
        ),
    )
    joined, moments = call(
        form_kernel, (rounded, shape(F32, 8, cols)), (share, both, field2, received2, near2)
    )
    moments = sum_over(moments, "asset")
    q2 = near(joined)
    partial = call(cross_third_kernel, field, (band, known, near2, far2))
    return call(
        combine_kernel,
        (out, out),
        (shift, moments, targets, rows1, rows2, partial, q2),
        scratch=[
            pltpu.VMEM((2, assets, cols), F32),
            pltpu.SemaphoreType.DMA((2, rows // 2)),
        ],
        results=HBM,
    )


def solution(mesh):
    return jax.shard_map(
        shards,
        mesh=mesh,
        in_specs=(
            P("asset", "rhs"),
            P("asset"),
            P("asset", None, "rhs", None),
            P("asset", None),
            P("asset"),
        ),
        out_specs=(P("asset", "rhs"), P("asset", "rhs")),
        check_vma=False,
    )
```

```python
import jax
import jax.numpy as jnp
from jax import lax
from jax.experimental import pallas as pl
from jax.experimental.pallas import tpu as pltpu
from jax.sharding import PartitionSpec as P

F32 = jnp.float32
BF16 = jnp.bfloat16
VMEM = pl.BlockSpec(memory_space=pltpu.VMEM)
SMEM = pl.BlockSpec(memory_space=pltpu.SMEM)
LIMIT = 8 * 1024 * 1024
HBM = pl.BlockSpec(memory_space=pltpu.HBM)
NN = (((1,), (0,)), ((), ()))
NT = (((1,), (1,)), ((), ()))


def call(kernel, out_shape, args, smem=0, outside=(), scratch=(), aliases=None, flops=0, results=VMEM):
    specs = [SMEM] * smem + [VMEM] * (len(args) - smem)
    for at in outside:
        specs[at] = HBM
    return pl.pallas_call(
        kernel,
        out_shape=out_shape,
        in_specs=specs,
        out_specs=jax.tree.map(lambda _: results, out_shape),
        scratch_shapes=scratch,
        input_output_aliases=aliases or {},
        cost_estimate=pl.CostEstimate(flops=flops, bytes_accessed=2**20, transcendentals=0) if flops else None,
        compiler_params=pltpu.CompilerParams(vmem_limit_bytes=LIMIT),
    )(*args)


def column_sums(values, width):
    folded = values[:, :width]
    for at in range(width, values.shape[1], width):
        folded = folded + values[:, at : at + width]
    return jnp.sum(folded.T, axis=0, keepdims=True)


def prepare_kernel(targets_ref, base_ref, rounded_ref, moment_ref):
    assets = targets_ref.shape[0]
    width = moment_ref.shape[1]
    for at in range(0, assets, width):
        tile = targets_ref[at : at + width, :].T
        base_ref[:, at : at + width] = tile
        rounded_ref[:, at : at + width] = tile.astype(BF16)
    values = targets_ref[...]
    moment_ref[...] = jnp.sum(values * values, axis=0, keepdims=True)


def place_blocks(col_ref, length_ref, offset, part_ref, band_ref):
    rows, slots, height, width = part_ref.shape
    spare = band_ref.shape[0] - 1
    total = rows * lax.axis_size("asset")
    first = lax.axis_index("asset") * rows - rows

    def one_row(row, carry):
        at = pl.ds(pl.multiple_of(row * width + offset, height), height)
        for slot in range(slots):
            place = col_ref[row, slot] - first
            place = jnp.where(place < 0, place + total, place)
            place = jnp.where(place >= total, place - total, place)
            place = jnp.where(slot < length_ref[row], place, spare)
            band_ref[place, at, :] = part_ref[row, slot]
        return carry

    lax.fori_loop(0, rows, one_row, 0)


def spread_first_kernel(col_ref, length_ref, part_ref, ridge_ref, band_ref, mean_ref):
    mean = jnp.sum(ridge_ref[...], axis=1, keepdims=True) / ridge_ref.shape[1]
    mean_ref[...] = jnp.broadcast_to(mean, mean_ref.shape)
    band_ref[...] = jnp.zeros_like(band_ref)
    height = part_ref.shape[2]
    mine = 0 if height == part_ref.shape[3] else lax.axis_index("rhs") * height
    place_blocks(col_ref, length_ref, mine, part_ref, band_ref)


def spread_other_kernel(col_ref, length_ref, part_ref, _, band_ref):
    height = part_ref.shape[2]
    place_blocks(col_ref, length_ref, (1 - lax.axis_index("rhs")) * height, part_ref, band_ref)


def is_odd(dims):
    return jnp.full(dims, lax.axis_index("asset") % 2, jnp.int32) == 1


def columns(ref, first, last, rows):
    return jnp.concatenate([ref[c, rows, :] for c in range(first, last)], axis=1)


def products_kernel(band_ref, v_ref, near_ref, far_ref):
    places, _, width = band_ref.shape
    rows = places // 3
    cols = v_ref.shape[0]
    odd = is_odd((cols, 2 * width))
    for j in range(0, rows, 2):
        out = slice(j * width, (j + 2) * width)
        low = slice(0, (j + 2) * width)
        high = slice(j * width, rows * width)
        before = lax.dot_general(
            v_ref[:, low], columns(band_ref, j, j + 2, low), NN, preferred_element_type=F32
        )
        after = lax.dot_general(
            v_ref[:, high],
            columns(band_ref, 2 * rows + j, 2 * rows + j + 2, high),
            NN,
            preferred_element_type=F32,
        )
        near_ref[:cols, out] = jnp.where(odd, before, after).astype(BF16)
        far_ref[:cols, out] = jnp.where(odd, after, before).astype(BF16)


def products_first_kernel(band_ref, v_ref, ridge_ref, near_ref, far_ref):
    products_kernel(band_ref, v_ref, near_ref, far_ref)
    cols, assets = v_ref.shape
    mean = jnp.sum(ridge_ref[...], axis=1, keepdims=True) / assets
    rest = jnp.broadcast_to(mean, (near_ref.shape[0] - cols, assets)).astype(BF16)
    near_ref[cols:, :] = rest
    far_ref[cols:, :] = rest


def products_second_kernel(band_ref, v_ref, mean_ref, near_ref, far_ref):
    products_kernel(band_ref, v_ref, near_ref, far_ref)
    cols = v_ref.shape[0]
    rest = (far_ref.shape[0] - cols, far_ref.shape[1])
    far_ref[cols:, :] = jnp.broadcast_to(mean_ref[0:1, 0:1], rest).astype(BF16)


def local_kernel(band_ref, v_ref, out_ref):
    places, _, width = band_ref.shape
    rows = places // 3
    cols = out_ref.shape[0]
    every = slice(0, rows * width)
    for j in range(0, rows, 2):
        out = slice(j * width, (j + 2) * width)
        out_ref[:, out] = lax.dot_general(
            v_ref[:cols, :],
            columns(band_ref, rows + j, rows + j + 2, every),
            NN,
            preferred_element_type=F32,
        ) + lax.dot_general(
            v_ref[:cols, :], columns(band_ref, rows, 2 * rows, out), NT, preferred_element_type=F32
        )


def neighbours(near_ref, far_ref, cols):
    near, far = near_ref[:cols, :].astype(F32), far_ref[:cols, :].astype(F32)
    odd = is_odd(near.shape)
    return jnp.where(odd, near, far).astype(BF16), jnp.where(odd, far, near).astype(BF16)


def forward_products(band_ref, before, after, j):
    places, _, width = band_ref.shape
    rows = places // 3
    out = slice(j * width, (j + 2) * width)
    return out, lax.dot_general(
        before[:, j * width :], columns(band_ref, j, rows, out), NT, preferred_element_type=F32
    ), lax.dot_general(
        after[:, : (j + 2) * width],
        columns(band_ref, 2 * rows, 2 * rows + j + 2, out),
        NT,
        preferred_element_type=F32,
    )


def gather_first_kernel(ridge_ref, k_ref, local_ref, own_ref, near_ref, far_ref, sum_ref, mean_ref):
    cols, width = k_ref.shape[0], mean_ref.shape[1]
    means = [ref[cols : cols + 16, :width].astype(F32)[:1] for ref in (own_ref, near_ref, far_ref)]
    odd = is_odd(means[0].shape)
    means += [jnp.where(odd, means[1], means[2]), jnp.where(odd, means[2], means[1])]
    means.append(means[0] + means[1])
    for i, value in enumerate(means):
        mean_ref[i : i + 1, :] = value
    both = local_ref[...] + near_ref[:cols, :].astype(F32) + far_ref[:cols, :].astype(F32)
    sum_ref[...] = ridge_ref[...] * k_ref[...] + 0.5 * both


def cross_first_kernel(
    band_ref, sum_ref, k_ref, mean_ref, near_ref, far_ref, next_ref, rounded_ref, before_ref, after_ref
):
    before, after = neighbours(near_ref, far_ref, k_ref.shape[0])
    for j in range(0, band_ref.shape[0] // 3, 2):
        out, first, second = forward_products(band_ref, before, after, j)
        before_ref[:, out] = first
        after_ref[:, out] = second
        value = sum_ref[:, out] + 0.5 * (first + second)
        next_ref[:, out] = value
        rounded_ref[:, out] = (value - mean_ref[0:1, 0:1] * k_ref[:, out]).astype(BF16)


def cross_second_kernel(
    band_ref, ridge_ref, mean_ref, k_ref, local0_ref, local_ref, before0_ref, after0_ref, qn0_ref, qf0_ref,
    near_ref, far_ref, sum_ref, before_ref, after_ref
):
    own, mean_near, mean_far, mean_before, mean_after = (mean_ref[i : i + 1, 0:1] for i in range(5))
    before, after = neighbours(near_ref, far_ref, k_ref.shape[0])
    for j in range(0, band_ref.shape[0] // 3, 2):
        out, first, second = forward_products(band_ref, before, after, j)
        before_ref[:, out] = first
        after_ref[:, out] = second
        known = own * local0_ref[:, out] + mean_before * before0_ref[:, out] + mean_after * after0_ref[:, out]
        known = known + mean_near * qn0_ref[: k_ref.shape[0], out].astype(F32) + mean_far * qf0_ref[: k_ref.shape[0], out].astype(F32)
        both = local_ref[:, out] + first + second + known
        sum_ref[:, out] = ridge_ref[:, out] * k_ref[:, out] + 0.5 * both


def finish_second_kernel(
    k0_ref, k_ref, mean_ref, sum_ref, own_ref, q_ref, next_ref, rounded_ref, total_ref
):
    cols, width = k_ref.shape[0], total_ref.shape[1]
    sums = [ref[cols : cols + 16, :width].astype(F32)[:1] for ref in (own_ref, q_ref)]
    total_ref[...] = sums[0] + sums[1]
    value = sum_ref[...] + 0.5 * q_ref[:cols, :].astype(F32)
    next_ref[...] = value
    own = mean_ref[0:1, 0:1]
    rounded_ref[...] = (value - 2 * own * k_ref[...] + own * own * k0_ref[...]).astype(BF16)


def settle_kernel(
    shift_ref, mean_ref, ridge_ref, k0_ref, k1_ref, k2_ref, local0_ref, local1_ref, local2_ref,
    before0_ref, before1_ref, after0_ref, after1_ref, qn0_ref, qf0_ref,
    m0_ref, to2_ref, to1_ref, r1_ref, near1_ref, near0_ref,
    sum_ref, rows1_ref, rows2_ref, moment_ref, both_ref, field_ref
):
    cols, width = k0_ref.shape[0], moment_ref.shape[1]
    c = shift_ref[0:1, 0:1]
    own, mean_near, mean_far, mean_before, mean_after = (mean_ref[i : i + 1, 0:1] - c for i in range(5))
    other = r1_ref[cols : cols + 16, :width].astype(F32)[:1, :1] - c
    totals = [jnp.zeros((cols, width), F32)] * 5
    for at in range(0, k0_ref.shape[1], width):
        out = slice(at, at + width)
        k0, k1 = k0_ref[:, out], k1_ref[:, out]
        s1 = k1 - c * k0
        s2 = k2_ref[:, out] - 2 * c * k1 + c * c * k0
        rows1_ref[out, :] = s1.T
        rows2_ref[out, :] = s2.T
        local = local2_ref[:, out] + 2 * own * local1_ref[:, out] + own * own * local0_ref[:, out]
        mine = (ridge_ref[:, out] - c) * s2 + 0.5 * local
        known = 2 * mean_before * before1_ref[:, out] + mean_before * mean_before * before0_ref[:, out]
        known = known + 2 * mean_after * after1_ref[:, out] + mean_after * mean_after * after0_ref[:, out]
        back = mean_near * mean_near * qn0_ref[:cols, out].astype(F32)
        back = back + mean_far * mean_far * qf0_ref[:cols, out].astype(F32)
        sum_ref[:, out] = mine + 0.5 * (known + back)
        both = to2_ref[:, out].astype(F32) + 2 * own * to1_ref[:, out].astype(F32)
        both_ref[:, out] = both + 2 * other * r1_ref[:cols, out].astype(F32)
        field = 2 * mean_near * near1_ref[:, out].astype(F32)
        field_ref[:, out] = field + mean_near * mean_near * near0_ref[:, out].astype(F32)
        parts = (k0 * s1, s1 * s1, s1 * s2, s2 * s2, s2 * (mine + back))
        totals = [total + part for total, part in zip(totals, parts, strict=True)]
    moment_ref[0:1, :] = m0_ref[...]
    for i, total in enumerate(totals):
        moment_ref[i + 1 : i + 2, :] = jnp.sum(total.T, axis=0, keepdims=True)
    moment_ref[6:8, :] = jnp.zeros((2, width), F32)


def form_kernel(share_ref, both_ref, field_ref, received_ref, near_ref, q_ref, moment_ref):
    cols, assets = both_ref.shape
    width = moment_ref.shape[1]
    total = jnp.zeros((cols, width), F32)
    for at in range(0, assets, width):
        out = slice(at, at + width)
        both = both_ref[:, out] + received_ref[:, out].astype(F32)
        q_ref[:, out] = both.astype(BF16)
        total = total + both * (field_ref[:, out] + near_ref[:, out].astype(F32))
    moment_ref[...] = share_ref[...]
    moment_ref[5:6, :] = share_ref[5:6, :] + jnp.sum(total.T, axis=0, keepdims=True)


def ratio(above, below):
    return jnp.where(below == 0, 0.0, above / below)


def scalars(m, shift, iters):
    zero = jnp.zeros_like(m[0])
    solution = [zero] * iters
    residual = [zero + 1.0] + [zero] * iters
    direction = [zero + 1.0] + [zero] * (iters - 1)

    def inner(a, b):
        total = zero
        for i, left in enumerate(a):
            for j, right in enumerate(b):
                if i + j < len(m):
                    total = total + left * right * m[i + j]
        return total

    now = m[0]
    for step in range(iters):
        used = direction[: step + 1]
        image = [shift * value for value in used] + [zero]
        for i, value in enumerate(used):
            image[i + 1] = image[i + 1] + value
        alpha = ratio(now, inner(used, image))
        for i, value in enumerate(used):
            solution[i] = solution[i] + alpha * value
        for i, value in enumerate(image):
            residual[i] = residual[i] - alpha * value
        if step + 1 < iters:
            left = residual[: step + 2]
            new = inner(left, left)
            beta = ratio(new, now)
            direction = [r + beta * d for r, d in zip(residual[:iters], direction, strict=True)]
            now = new
    return solution, residual


def combine_kernel(
    shift_ref, moment_ref, targets_ref, k1_ref, k2_ref, band_ref, known_ref, near_ref, far_ref, q_ref,
    solution_hbm, residual_hbm, held, sems
):
    cols, width = known_ref.shape[0], moment_ref.shape[1]
    m = [moment_ref[i : i + 1, :] for i in range(6)]
    x, r = scalars(m, shift_ref[0:1, :], 3)
    size = 2 * width
    parts = range(targets_ref.shape[0] // size)
    copies = []

    def leave(kind, target, part, out):
        copy = pltpu.make_async_copy(held.at[kind, out, :], target.at[out, :], sems.at[kind, part])
        copy.start()
        copies.append(copy)

    for part in parts:
        out = slice(part * size, (part + 1) * size)
        k0, k1, k2 = targets_ref[out, :], k1_ref[out, :], k2_ref[out, :]
        held[0, out, :] = x[0] * k0 + x[1] * k1 + x[2] * k2
        leave(0, solution_hbm, part, out)
    before, after = neighbours(near_ref, far_ref, cols)
    for part in parts:
        out, first, second = forward_products(band_ref, before, after, 2 * part)
        k3 = (known_ref[:, out] + 0.5 * (first + second + q_ref[:, out].astype(F32))).T
        k0, k1, k2 = targets_ref[out, :], k1_ref[out, :], k2_ref[out, :]
        held[1, out, :] = r[0] * k0 + r[1] * k1 + r[2] * k2 + r[3] * k3
        leave(1, residual_hbm, part, out)
    for copy in copies:
        copy.wait()


def near(value):
    count = lax.axis_size("asset")
    return lax.ppermute(value, "asset", [(i, i ^ 1) for i in range(count)])


def far(value):
    count = lax.axis_size("asset")
    return lax.ppermute(
        value, "asset", [(i, (i + 1 if i % 2 else i - 1) % count) for i in range(count)]
    )


def forward(value):
    count = lax.axis_size("asset")
    return lax.ppermute(
        value, "asset", [(i, (i - 2 if i % 2 else i + 2) % count) for i in range(count)]
    )


def back(value):
    count = lax.axis_size("asset")
    return lax.ppermute(
        value, "asset", [(i, (i + 2 if i % 2 else i - 2) % count) for i in range(count)]
    )


def add_kernel(near_ref, received_ref, mean_ref, out_ref):
    cols = near_ref.shape[0]
    out_ref[:cols, :] = (near_ref[...].astype(F32) + received_ref[:cols, :].astype(F32)).astype(BF16)
    rest = (out_ref.shape[0] - cols, out_ref.shape[1])
    out_ref[cols:, :] = jnp.broadcast_to(mean_ref[0:1, 0:1], rest).astype(BF16)


def sum_step(value, axis, distance):
    count = lax.axis_size(axis)
    return value + lax.ppermute(value, axis, [(i, i ^ distance) for i in range(count)])


def sum_over(value, axis):
    count = lax.axis_size(axis)
    step = 1
    while step < count:
        total = value
        for distance in (step, 2 * step, 3 * step) if 2 * step < count else (step,):
            route = [(i, i ^ distance) for i in range(count)]
            total = total + lax.ppermute(value, axis, route)
        value = total
        step *= 4
    return value


def together(*values):
    return lax.optimization_barrier(values)


def shards(targets, ridge, blocks, col_index, row_length):
    rows, slots, height, width = blocks.shape
    cols = targets.shape[1]
    assets = rows * width
    devices = lax.axis_size("asset")
    halves = lax.axis_size("rhs")
    ridge = ridge[None, :]

    def shape(kind, *dims):
        return jax.ShapeDtypeStruct(dims, kind)

    field, rounded, row = shape(F32, cols, assets), shape(BF16, cols, assets), shape(F32, 1, cols)
    band_shape = shape(BF16, 3 * rows + 1, assets, width)
    if halves == 2:
        part, other = blocks, lax.ppermute(blocks, "rhs", [(0, 1), (1, 0)])
    else:
        part, other = lax.all_gather(blocks, "rhs", axis=2, tiled=True), None

    k0, v0, m0 = call(prepare_kernel, (field, rounded, row), (targets,), flops=5 * 10**9)
    near0 = near(v0)
    band, mean = call(
        spread_first_kernel,
        (band_shape, shape(F32, 1, width)),
        (col_index, row_length, part, ridge),
        smem=2,
    )
    if other is not None:
        band = call(
            spread_other_kernel, band_shape, (col_index, row_length, other, band), smem=2, aliases={3: 0}
        )
    distances = [1 << i for i in range(1, (devices - 1).bit_length())]
    pieces, message = (field,) * 3, shape(BF16, cols + 16, assets)

    to_near, to_far = call(products_first_kernel, (message,) * 2, (band, v0, ridge))
    qf0, qn0 = far(to_far), near(to_near)
    local0 = call(local_kernel, field, (band, together(v0, to_near)[0]))
    far0 = forward(together(near0, local0)[0])
    mean = together(mean, local0)[0]
    for distance in distances[1:-1]:
        mean = sum_step(mean, "asset", distance)
    mean, local0 = together(mean, local0)
    partial, means = call(
        gather_first_kernel, (field, shape(F32, 8, width)), (ridge, k0, local0, to_near, qn0, qf0)
    )
    k1, v1, before0, after0 = call(
        cross_first_kernel, (field, rounded, field, field), (band, partial, k0, means, near0, far0)
    )

    to_near1, to_far1 = call(products_second_kernel, (rounded, message), (band, v1, means))
    received, near1 = back(to_far1), near(v1)
    far1 = forward(near1)
    mean = sum_step(together(mean, to_near1)[0], "asset", distances[0])
    joined = call(add_kernel, message, (to_near1, received, mean))
    q1 = near(joined)
    local1 = call(local_kernel, field, (band, v1))
    partial, before1, after1 = call(
        cross_second_kernel,
        pieces,
        (band, ridge, means, k1, local0, local1, before0, after0, qn0, qf0, near1, far1),
    )
    k2, v2, mean = call(
        finish_second_kernel,
        (field, rounded, shape(F32, 1, width)),
        (k0, k1, means, partial, joined, q1),
    )

    to_near2, to_far2 = call(products_kernel, (rounded,) * 2, (band, v2))
    received2 = back(to_far2)
    local2 = call(local_kernel, field, (band, together(v2, to_near2)[0]), flops=5 * 10**9)
    near2 = near(together(v2, local2)[0])
    far2 = forward(near2)
    shift = sum_step(mean, "asset", distances[-1]) / devices
    out = shape(F32, assets, cols)
    known, rows1, rows2, share, both, field2 = call(
        settle_kernel,
        (field, out, out, shape(F32, 8, cols), field, field),
        (
            shift, means, ridge, k0, k1, k2, local0, local1, local2,
            before0, before1, after0, after1, qn0, qf0,
            m0, to_near2, to_near1, received, near1, near0,
        ),
    )
    joined, moments = call(
        form_kernel, (rounded, shape(F32, 8, cols)), (share, both, field2, received2, near2)
    )
    moments = sum_over(moments, "asset")
    q2 = near(joined)
    return call(
        combine_kernel,
        (out, out),
        (shift, moments, targets, rows1, rows2, band, known, near2, far2, q2),
        scratch=[
            pltpu.VMEM((2, assets, cols), F32),
            pltpu.SemaphoreType.DMA((2, rows // 2)),
        ],
        results=HBM,
    )


def solution(mesh):
    return jax.shard_map(
        shards,
        mesh=mesh,
        in_specs=(
            P("asset", "rhs"),
            P("asset"),
            P("asset", None, "rhs", None),
            P("asset", None),
            P("asset"),
        ),
        out_specs=(P("asset", "rhs"), P("asset", "rhs")),
        check_vma=False,
    )
```
